256 devices in a mesh: blk: 128 (over z, x, y), cols: 2 (over core).
Axes of the slice: x: 4, y: 4, z: 8, core: 2. Of those that a mesh axis runs over, the one named last changes fastest.
Arguments:
- rhs: bfloat16 [2048, 128, 512], P('blk', None, 'cols'), parts along dimension 2, may hold values from -6 to 6
- diag_inverse: bfloat16 [2048, 128, 128], P('blk')
- lower_blocks: bfloat16 [2048, 2, 128, 128], P('blk'), may hold values from -0.25 to 0.25
- local_cols: int32 [2048, 2], P('blk'), may hold values from 0 to 14, as said below
- sep_rhs: bfloat16 [128, 384, 512], P('blk', None, 'cols'), parts along dimension 2, may hold values from -6 to 6
- sep_blocks: bfloat16 [128, 8, 2, 384, 128], P('blk')
- sep_cols: int32 [128, 8, 2], P('blk'), may hold values from 0 to 15
- sep_inverse: bfloat16 [128, 384, 384], P('blk')
- sep_link: bfloat16 [128, 384, 384], P('blk'), may hold values from -0.21875 to 0.21875
Outputs:
- solution: bfloat16 [2048, 128, 512], P('blk', None, 'cols'), parts along dimension 2
- sep_solution: bfloat16 [128, 384, 512], P('blk', None, 'cols'), parts along dimension 2
The draws below stay inside these ranges and needn't reach their ends.
There are 2 independent parts, one for each index of `cols`. The reference program is written for one: setup_inputs(seed, part) draws one part's arguments, and reference() takes and returns one part's arrays. A program takes and returns all parts, laid end to end along the dimension named above; an argument that names none is the same for every part. Nothing has to cross between parts.
Inputs may be any that keep to these rules, and one draw needn't show every extreme that they name: `local_cols`: subtree row r of a device names its block r - 1 first and a block below r - 1 second; both are 0 for r < 2.
All inputs are finite; a program needn't handle non-finite values.
Results may differ from the reference program's by a relative error of at most 0.015.
Values may be sent and summed in bfloat16 or wider, within the bound.
No kernel may reach another device: no remote copies, remote signals or barrier semaphores. Data moves between devices by JAX's collectives and lax.ppermute only.
A program may use at most 64 MiB of HBM per device.

```python
import math
import jax
import jax.numpy as jnp
from jax import lax

B = 128
SW = 384
SAMPLES = 256
LOC = 16
NNZ = 2
SEP_NNZ = 2
NODES = 128
LEV = 7
NLEV = 8
BLOCK_ROWS = 2048


def triangle(key, shape, factor):
    key_diag, key_lower = jax.random.split(key)
    width = shape[-1]
    diagonal = jax.random.uniform(key_diag, shape[:-1], jnp.float32, 0.5, 1.0)
    lower_part = jax.random.normal(key_lower, shape, jnp.float32) * (0.4 / math.sqrt(width))
    row_ids = lax.broadcasted_iota(jnp.int32, (width, width), 0)
    column_ids = lax.broadcasted_iota(jnp.int32, (width, width), 1)
    result = jnp.where(row_ids > column_ids, lower_part, 0.0) + jnp.where(row_ids == column_ids, 1.0, 0.0) * diagonal[..., None]
    return result * factor


def draw_diag_inverse(key, part):
    key = jax.random.fold_in(key, 11)
    return triangle(key, (BLOCK_ROWS, B, B), 1.0).astype(jnp.bfloat16)


def draw_sep_inverse(key, part):
    key = jax.random.fold_in(key, 12)
    return triangle(key, (NODES, SW, SW), 0.7).astype(jnp.bfloat16)


def draw_local_cols(key, part):
    key = jax.random.fold_in(key, 13)
    row_ids = jnp.arange(BLOCK_ROWS, dtype=jnp.int32) % LOC
    previous = jnp.maximum(row_ids - 1, 0)
    random_bits = jax.random.randint(key, (BLOCK_ROWS,), 0, 1 << 20, dtype=jnp.int32)
    earlier = random_bits % jnp.maximum(row_ids - 1, 1)
    return jnp.stack([previous, earlier], axis=1).astype(jnp.int32)


def draw_sep_blocks(key, part):
    key = jax.random.fold_in(key, 14)
    level_ids = jnp.arange(NLEV, dtype=jnp.int32) + 1
    span = (2.0 ** jnp.minimum(level_ids, LEV)).astype(jnp.float32)
    factor = 0.8 / jnp.sqrt(span * SEP_NNZ * B)
    values = jax.random.normal(key, (NODES, NLEV, SEP_NNZ, SW, B), jnp.float32)
    return (values * factor[None, :, None, None, None]).astype(jnp.bfloat16)


def place_ends(values, key, low, top_value):
    shape = values.shape
    spot = [jax.random.randint(jax.random.fold_in(key, axis), (), 0, shape[axis]) for axis in range(len(shape))]
    values = values.at[tuple(spot)].set(low)
    longest = shape.index(max(shape))
    spot[longest] = (spot[longest] + 1) % shape[longest]
    return values.at[tuple(spot)].set(top_value)


def block_scale(rng, dims, shards, least, top_value):
    factor_of, own = 1.0, jax.random.fold_in(rng, 6)
    for dim, shards_of in shards:
        draws = jnp.exp(jax.random.uniform(jax.random.fold_in(own, dim), (shards_of,), jnp.float32, least / len(shards), top_value / len(shards)))
        factor_of = factor_of * jnp.repeat(draws, dims[dim] // shards_of).reshape([-1 if axis == dim else 1 for axis in range(len(dims))])
    return factor_of


def bell_draw(key, extent, spread, limit, shards=(), kind=jnp.bfloat16):
    entries = jax.random.normal(key, extent, jnp.float32) * spread
    if len(shards) > 0:
        entries = block_scale(key, extent, shards, -0.22, 0.18) * entries
    return jnp.clip(entries, min=-limit, max=limit).astype(kind)


def setup_inputs(seed: int = 0, part: int = 0) -> dict:
    key_list = jax.random.split(jax.random.key(seed), 10)
    part_splits = jax.random.split(jax.random.fold_in(key_list[9], part), 10)
    return {
        "rhs": bell_draw(part_splits[0], (BLOCK_ROWS, B, SAMPLES), 1.0, 6.0, ((0, 128),)),
        "diag_inverse": draw_diag_inverse(jax.random.fold_in(key_list[9], 71), part),
        "lower_blocks": bell_draw(key_list[2], (BLOCK_ROWS, NNZ, B, B), (4 * B) ** -0.5, 0.25, ((0, 128),)),
        "local_cols": draw_local_cols(jax.random.fold_in(key_list[9], 71), part),
        "sep_rhs": bell_draw(part_splits[4], (NODES, SW, SAMPLES), 1.0, 6.0, ((0, 128),)),
        "sep_blocks": draw_sep_blocks(jax.random.fold_in(key_list[9], 71), part),
        "sep_cols": place_ends(jax.random.randint(key_list[6], (NODES, NLEV, SEP_NNZ), 0, LOC), jax.random.fold_in(key_list[6], 1), 0, LOC - 1).astype(jnp.int32),
        "sep_inverse": draw_sep_inverse(jax.random.fold_in(key_list[9], 71), part),
        "sep_link": bell_draw(key_list[8], (NODES, SW, SW), (2 * SW) ** -0.5, 0.21875, ((0, 128),)),
    }


def rounded(values):
    return lax.optimization_barrier(values.astype(jnp.bfloat16)).astype(jnp.float32)


def apply_all(matrices, vectors):
    return jnp.einsum("nij,njs->nis", matrices.astype(jnp.float32), vectors.astype(jnp.float32))


def apply_transposed(matrices, vectors):
    return jnp.einsum("nji,njs->nis", matrices.astype(jnp.float32), vectors.astype(jnp.float32))


def owners_of(level):
    count = max(NODES >> level, 1)
    return jnp.arange(count, dtype=jnp.int32) * (2 ** level) + (2 ** (level - 1) - 1)


def reference(rhs, diag_inverse, lower_blocks, local_cols, sep_rhs, sep_blocks, sep_cols, sep_inverse, sep_link):
    rhs_tiles = rhs.reshape(NODES, LOC, B, SAMPLES)
    inverse_tiles = diag_inverse.reshape(NODES, LOC, B, B)
    lower_tiles = lower_blocks.reshape(NODES, LOC, NNZ, B, B)
    column_tiles = local_cols.reshape(NODES, LOC, NNZ)
    node_ids = jnp.arange(NODES, dtype=jnp.int32)

    def forward_row(row, solved):
        lower_row = lax.dynamic_index_in_dim(lower_tiles, row, 1, keepdims=False)
        column_row = lax.dynamic_index_in_dim(column_tiles, row, 1, keepdims=False)
        update = jnp.zeros((NODES, B, SAMPLES), jnp.float32)
        for slot in range(NNZ):
            update = update + apply_all(lower_row[:, slot], solved[node_ids, column_row[:, slot]])
        target = rounded(lax.dynamic_index_in_dim(rhs_tiles, row, 1, keepdims=False).astype(jnp.float32) - update)
        value = apply_all(lax.dynamic_index_in_dim(inverse_tiles, row, 1, keepdims=False), target).astype(jnp.bfloat16)
        return lax.dynamic_update_index_in_dim(solved, value, row, 1)

    solved = lax.fori_loop(0, LOC, forward_row, jnp.zeros((NODES, LOC, B, SAMPLES), jnp.bfloat16))

    pattern = (node_ids ^ (node_ids + 1)) + 1
    partials = []
    for level_idx in range(NLEV):
        total_part = jnp.zeros((NODES, SW, SAMPLES), jnp.float32)
        for slot in range(SEP_NNZ):
            total_part = total_part + apply_all(sep_blocks[:, level_idx, slot], solved[node_ids, sep_cols[:, level_idx, slot]])
        owned = (pattern == 2 ** (level_idx + 1))[:, None, None]
        total_part = total_part - jnp.where(owned, sep_rhs.astype(jnp.float32), 0.0)
        partials.append(total_part)

    node_values = []
    for level in range(1, NLEV + 1):
        span = 2 ** min(level, LEV)
        count = NODES // span
        total = partials[level - 1].reshape(count, span, SW, SAMPLES).sum(axis=1)
        if level >= 2:
            child_terms = apply_all(sep_link[owners_of(level - 1)], node_values[-1])
            total = total + child_terms.reshape(count, -1, SW, SAMPLES).sum(axis=1)
        value = apply_all(sep_inverse[owners_of(level)], rounded(-total)).astype(jnp.bfloat16)
        node_values.append(value)

    back_values = [None] * NLEV
    back_values[NLEV - 1] = apply_transposed(sep_inverse[owners_of(NLEV)], node_values[NLEV - 1]).astype(jnp.bfloat16)
    for level in range(NLEV - 1, 0, -1):
        count = NODES >> level
        parent_rep = back_values[level][jnp.arange(count, dtype=jnp.int32) // 2]
        target = rounded(node_values[level - 1].astype(jnp.float32) - apply_transposed(sep_link[owners_of(level)], parent_rep))
        back_values[level - 1] = apply_transposed(sep_inverse[owners_of(level)], target).astype(jnp.bfloat16)

    sep_solution = jnp.zeros((NODES, SW, SAMPLES), jnp.bfloat16)
    for level in range(1, NLEV + 1):
        sep_solution = sep_solution.at[owners_of(level)].set(back_values[level - 1])

    pending = jnp.zeros((NODES, LOC, B, SAMPLES), jnp.float32)
    for level_idx in range(NLEV):
        ancestor = back_values[level_idx][node_ids >> (level_idx + 1)]
        for slot in range(SEP_NNZ):
            contrib = apply_transposed(sep_blocks[:, level_idx, slot], ancestor)
            pending = pending.at[node_ids, sep_cols[:, level_idx, slot]].add(contrib)

    def backward_row(step_no, carry):
        solution, pending = carry
        row = LOC - 1 - step_no
        target = rounded(lax.dynamic_index_in_dim(solved, row, 1, keepdims=False).astype(jnp.float32) - lax.dynamic_index_in_dim(pending, row, 1, keepdims=False))
        value = apply_transposed(lax.dynamic_index_in_dim(inverse_tiles, row, 1, keepdims=False), target).astype(jnp.bfloat16)
        solution = lax.dynamic_update_index_in_dim(solution, value, row, 1)
        lower_row = lax.dynamic_index_in_dim(lower_tiles, row, 1, keepdims=False)
        column_row = lax.dynamic_index_in_dim(column_tiles, row, 1, keepdims=False)
        for slot in range(NNZ):
            pending = pending.at[node_ids, column_row[:, slot]].add(apply_transposed(lower_row[:, slot], value))
        return solution, pending

    solution, pending = lax.fori_loop(0, LOC, backward_row, (jnp.zeros((NODES, LOC, B, SAMPLES), jnp.bfloat16), pending))
    return solution.reshape(BLOCK_ROWS, B, SAMPLES), sep_solution
```

```python
import jax
import jax.numpy as jnp
from jax import lax
from jax.experimental import pallas as pl
from jax.experimental.pallas import tpu as pltpu
from jax.sharding import PartitionSpec as P

F32 = jnp.float32
BF16 = jnp.bfloat16
PLANE_BITS = 4
LOW = 3


def dot(left, right):
    return jnp.dot(left, right, preferred_element_type=F32)


def dot_t(left, right):
    return lax.dot_general(left, right, (((0,), (0,)), ((), ())), preferred_element_type=F32)


def dot_nt(left, right):
    return lax.dot_general(left, right, (((1,), (1,)), ((), ())), preferred_element_type=F32)


def in_vmem(kernel, outs, scalars, arrays, scratch=(), flops=10**9):
    vmem = pl.BlockSpec(memory_space=pltpu.VMEM)
    smem = pl.BlockSpec(memory_space=pltpu.SMEM)
    moved = sum(a.size * a.dtype.itemsize for a in arrays)
    moved += sum(o.size * o.dtype.itemsize for o in outs)
    return pl.pallas_call(
        kernel,
        out_shape=tuple(outs),
        in_specs=[smem] * len(scalars) + [vmem] * len(arrays),
        out_specs=tuple(vmem for _ in outs),
        scratch_shapes=list(scratch),
        compiler_params=pltpu.CompilerParams(vmem_limit_bytes=48 * 2**20),
        cost_estimate=pl.CostEstimate(flops=flops, bytes_accessed=moved, transcendentals=0),
    )(*scalars, *arrays)


def shaped(shape, dtype):
    return jax.ShapeDtypeStruct(shape, dtype)


def whole(halves, index):
    return jnp.concatenate([halves[core, index] for core in range(halves.shape[0])], axis=0)


def gain_kernel(core, inverse, link, gains, full):
    own = inverse[...]
    full[0] = dot(link[...], own).astype(BF16)
    full[1] = dot_t(own, own).astype(BF16)
    rows = gains.shape[1]
    first = pl.multiple_of(core[0] * rows, rows)
    gains[0] = full[0, pl.ds(first, rows)]
    gains[1] = full[1, pl.ds(first, rows)]


def forward_kernel(cols, sep_cols, rhs, inverse, lower, sep_blocks, solved, partial, folded):
    rows, width, _ = rhs.shape
    for row in range(1, rows):
        pair = jnp.concatenate([lower[row, 0], lower[row, 1]], axis=1)
        folded[row] = dot(inverse[row], pair).astype(BF16)
    value = dot(inverse[0], rhs[0]).astype(BF16)
    solved[0] = value
    earlier = value
    for row in range(1, rows):
        base = dot(inverse[row], rhs[row]) - dot(folded[row, :, width:], earlier)
        if row + 1 < rows:
            earlier = solved[cols[row + 1, 1]]
        value = (base - dot(folded[row, :, :width], value)).astype(BF16)
        solved[row] = value
    for level in range(partial.shape[0]):
        pair = jnp.concatenate([sep_blocks[level, 0], sep_blocks[level, 1]], axis=1)
        sources = jnp.concatenate(
            [solved[sep_cols[level, 0]], solved[sep_cols[level, 1]]], axis=0
        )
        partial[level] = dot(pair, sources)


def path_kernel(own_level, partial, sep_rhs, gains, low, high):
    count = partial.shape[0]
    slices, _, slice_rows, _ = high.shape
    for level in range(count):
        total = partial[level]
        total = total - jnp.where(own_level[0] == level, sep_rhs[...].astype(F32), 0.0)
        if 1 <= level <= PLANE_BITS:
            total = total - dot(whole(gains, level - 1), value)
        value = total.astype(BF16)
        turned = value.T
        if level < LOW:
            low[level] = turned
        else:
            for piece in range(slices):
                rows = slice(piece * slice_rows, (piece + 1) * slice_rows)
                high[piece, level - LOW] = turned[rows]


def plane_kernel(arrived, gains, sums):
    for index in range(sums.shape[0]):
        total = arrived[0, index].astype(F32)
        for source in range(1, arrived.shape[0]):
            total = total + arrived[source, index].astype(F32)
        if index >= 2:
            total = total - dot_nt(value, whole(gains, index - 2))
        value = total.astype(BF16)
        sums[index] = total


def top_kernel(sums, finish, spread):
    for index in range(sums.shape[0]):
        value = -dot(sums[index].astype(BF16), whole(finish, index))
        value = value.astype(BF16)
        for piece in range(spread.shape[0]):
            spread[piece, index] = value


def prepare_kernel(cols, sep_cols, solved, inverse, lower, sep_blocks, start, chain, couple):
    rows = solved.shape[0]
    for row in range(rows):
        start[row] = dot_t(inverse[row], solved[row])
    for row in range(1, rows):
        for slot in range(2):
            column = cols[row, slot] if slot else row - 1
            chain[row, slot] = dot(lower[row, slot], inverse[column]).astype(BF16).T
    for level in range(sep_blocks.shape[0]):
        for slot in range(2):
            product = dot(sep_blocks[level, slot], inverse[sep_cols[level, slot]])
            couple[level, slot] = product.astype(BF16).T


def backward_kernel(
    cols,
    sep_cols,
    own_level,
    start,
    chain,
    couple,
    high,
    low1,
    low2,
    low3,
    finish,
    gains_low,
    gains_high,
    solution,
    own,
    pending,
    nodes,
):
    rows = start.shape[0]
    count = nodes.shape[0]
    lows = (low1, low2, low3)
    pending[...] = start[...]
    for level in range(count - 1, -1, -1):
        if level < LOW:
            node = -dot(lows[level][...], whole(finish, level))
        else:
            node = jnp.concatenate(
                [high[piece, level - LOW] for piece in range(high.shape[0])], axis=0
            ).astype(F32)
        if level + 1 < count:
            split = gains_low.shape[1]
            gain = whole(gains_low, level) if level < split else whole(gains_high, level - split)
            node = node - dot(vector, gain)
        vector = node.astype(BF16)
        nodes[level] = vector
        for slot in range(2):
            column = sep_cols[level, slot]
            pending[column] = pending[column] - dot_nt(couple[level, slot], vector)
    own[...] = nodes[own_level[0]].T
    following = pending[rows - 1]
    for row in range(rows - 1, -1, -1):
        value = following.astype(BF16)
        solution[row] = value
        if row:
            following = pending[row - 1] - dot(chain[row, 0], value)
            if row > 1:
                column = cols[row, 1]
                pending[column] = pending[column] - dot(chain[row, 1], value)
            else:
                following = following - dot(chain[row, 1], value)


def swap(value, mask):
    size = lax.axis_size("blk")
    return lax.ppermute(value, "blk", [(i, i ^ mask) for i in range(size)])


def per_device(
    rhs,
    diag_inverse,
    lower_blocks,
    local_cols,
    sep_rhs,
    sep_blocks,
    sep_cols,
    sep_inverse,
    sep_link,
):
    size = lax.axis_size("blk")
    device = lax.axis_index("blk")
    cores = lax.axis_size("cols")
    bits = size.bit_length() - 1
    count = bits + 1
    rows, width, columns = rhs.shape
    sep_width = sep_rhs.shape[1]
    plane = 1 << PLANE_BITS
    slice_rows = columns // plane
    sep_cols = sep_cols[0]
    sep_blocks = sep_blocks[0]
    own_level = sum(
        (((device + 1) & (2**k - 1)) == 0).astype(jnp.int32) for k in range(1, count)
    )[None]

    def step_mask(bit):
        base = 0 if bit < 2 else 2 if bit < 4 else 4
        return (2 << bit) - (1 << base)

    (gains,) = in_vmem(
        gain_kernel,
        [shaped((2, sep_width // cores, sep_width), BF16)],
        [lax.axis_index("cols")[None]],
        [sep_inverse[0], sep_link[0]],
        [pltpu.VMEM((2, sep_width, sep_width), BF16)],
    )

    def ancestors(top):
        found = []
        for bit in range(bits):
            arrived = swap(top, step_mask(bit))
            upper = (device >> bit & 1) == 1
            found.append(jnp.where(upper, arrived, top))
            top = jnp.where(upper, top, arrived)
        return found + [top]

    gain_list = ancestors(gains[0])
    finish_list = ancestors(gains[1])
    gains_low = lax.all_gather(jnp.stack(gain_list[:PLANE_BITS]), "cols")

    solved, partial = in_vmem(
        forward_kernel,
        [shaped(rhs.shape, BF16), shaped((count, sep_width, columns), F32)],
        [local_cols, sep_cols],
        [rhs, diag_inverse, lower_blocks, sep_blocks],
        [pltpu.VMEM((rows, width, 2 * width), BF16)],
    )
    start, chain, couple = in_vmem(
        prepare_kernel,
        [
            shaped(rhs.shape, F32),
            shaped((rows, 2, width, width), BF16),
            shaped((count, 2, width, sep_width), BF16),
        ],
        [local_cols, sep_cols],
        [solved, diag_inverse, lower_blocks, sep_blocks],
    )
    low, high = in_vmem(
        path_kernel,
        [
            shaped((LOW, columns, sep_width), BF16),
            shaped((plane, count - LOW, slice_rows, sep_width), BF16),
        ],
        [own_level],
        [partial, sep_rhs[0], gains_low],
    )

    def added(mine, arrived):
        return (mine.astype(F32) + arrived.astype(F32)).astype(BF16)

    lows = []
    rest = low
    for bit in range(LOW):
        rest = added(rest, swap(rest, step_mask(bit)))
        lows.append(rest[0])
        rest = rest[1:]

    groups = [[g * plane + i for i in range(plane)] for g in range(size // plane)]
    arrived = lax.all_to_all(high, "blk", 0, 0, axis_index_groups=groups, tiled=True)
    gains_high = lax.all_gather(jnp.stack(gain_list[PLANE_BITS:bits]), "cols")
    (sums,) = in_vmem(
        plane_kernel,
        [shaped((count - LOW, slice_rows, sep_width), F32)],
        [],
        [arrived, gains_high],
    )
    for bit in range(PLANE_BITS, bits):
        first = bit - LOW
        part = sums[first:]
        part = part + swap(part.astype(BF16), step_mask(bit)).astype(F32)
        sums = jnp.concatenate([sums[:first], part])
    finish = lax.all_gather(jnp.stack(finish_list), "cols")
    (spread,) = in_vmem(
        top_kernel,
        [shaped(high.shape, BF16)],
        [],
        [sums, finish[:, LOW:]],
    )
    values = lax.all_to_all(spread, "blk", 0, 0, axis_index_groups=groups, tiled=True)
    solution, own = in_vmem(
        backward_kernel,
        [shaped(rhs.shape, BF16), shaped((sep_width, columns), BF16)],
        [local_cols, sep_cols, own_level],
        [start, chain, couple, values, *lows, finish[:, :LOW], gains_low, gains_high],
        [pltpu.VMEM(rhs.shape, F32), pltpu.VMEM((count, columns, sep_width), BF16)],
    )
    return solution, own[None]


def solution(mesh):
    return jax.shard_map(
        per_device,
        mesh=mesh,
        in_specs=(
            P("blk", None, "cols"),
            P("blk", None, None),
            P("blk", None, None, None),
            P("blk", None),
            P("blk", None, "cols"),
            P("blk", None, None, None, None),
            P("blk", None, None),
            P("blk", None, None),
            P("blk", None, None),
        ),
        out_specs=(P("blk", None, "cols"), P("blk", None, "cols")),
        check_vma=False,
    )
```

```python
import jax
import jax.numpy as jnp
from jax import lax
from jax.experimental import pallas as pl
from jax.experimental.pallas import tpu as pltpu
from jax.sharding import PartitionSpec as P

F32 = jnp.float32
BF16 = jnp.bfloat16
PLANE_BITS = 4
LOW = 3


def dot(left, right):
    return jnp.dot(left, right, preferred_element_type=F32)


def dot_t(left, right):
    return lax.dot_general(left, right, (((0,), (0,)), ((), ())), preferred_element_type=F32)


def dot_nt(left, right):
    return lax.dot_general(left, right, (((1,), (1,)), ((), ())), preferred_element_type=F32)


def start_all(far, near, sems):
    copies = [pltpu.make_async_copy(far[i], near[i], sems.at[i]) for i in range(len(far))]
    for copy in copies:
        copy.start()
    return copies


def in_vmem(kernel, outs, scalars, arrays, scratch=()):
    counts = len(scalars), len(arrays), len(outs), len(arrays)

    def loaded(*refs):
        parts, first = [], 0
        for amount in counts:
            parts.append(refs[first : first + amount])
            first += amount
        small, far, results, near = parts
        for copy in start_all(far, near, refs[-1]):
            copy.wait()
        kernel(*small, *near, *results, *refs[first:-1])

    return placed(
        loaded,
        outs,
        scalars,
        arrays,
        [pltpu.VMEM(array.shape, array.dtype) for array in arrays]
        + list(scratch)
        + [pltpu.SemaphoreType.DMA((len(arrays),))],
    )


def placed(kernel, outs, scalars, arrays, scratch):
    vmem, smem = pl.BlockSpec(memory_space=pltpu.VMEM), pl.BlockSpec(memory_space=pltpu.SMEM)
    moved = sum(a.size * a.dtype.itemsize for a in arrays)
    moved += sum(o.size * o.dtype.itemsize for o in outs)
    return pl.pallas_call(
        kernel,
        out_shape=tuple(outs),
        in_specs=[smem] * len(scalars) + [pl.BlockSpec(memory_space=pl.ANY)] * len(arrays),
        out_specs=tuple(vmem for _ in outs),
        scratch_shapes=scratch,
        compiler_params=pltpu.CompilerParams(vmem_limit_bytes=56 * 2**20),
        cost_estimate=pl.CostEstimate(flops=10**9, bytes_accessed=moved, transcendentals=0),
    )(*scalars, *arrays)


def shaped(shape, dtype):
    return jax.ShapeDtypeStruct(shape, dtype)


def whole(core, mine, other, index):
    if mine.shape[1] == mine.shape[2]:
        return mine[index]
    first = core[0] == 0
    upper = jnp.where(first, mine[index], other[index])
    lower = jnp.where(first, other[index], mine[index])
    return jnp.concatenate([upper, lower], axis=0)


def gain_kernel(core, inverse, link, gain, finish, full):
    own = inverse[...]
    full[0] = dot(link[...], own).astype(BF16)
    full[1] = dot_t(own, own).astype(BF16)
    rows = gain.shape[0]
    first = pl.multiple_of(core[0] * rows, rows)
    gain[...] = full[0, pl.ds(first, rows)]
    finish[...] = full[1, pl.ds(first, rows)]


def spread_out(pieces, index, value):
    turned = value.T
    rows = pieces.shape[2]
    for piece in range(pieces.shape[0]):
        pieces[piece, index] = turned[piece * rows : (piece + 1) * rows]


def forward_kernel(
    cols,
    sep_cols,
    own_level,
    *refs,
):
    far, (solved, partial), near, (folded, sems) = refs[:5], refs[5:7], refs[7:12], refs[12:]
    inverse, lower, rhs, sep_blocks, sep_rhs = near
    copies = start_all(far, near, sems)
    copies[0].wait()
    copies[1].wait()
    rows, width, _ = rhs.shape
    for row in range(1, rows):
        pair = jnp.concatenate([lower[row, 0], lower[row, 1]], axis=1)
        folded[row] = dot(inverse[row], pair).astype(BF16)
    copies[2].wait()
    value = dot(inverse[0], rhs[0]).astype(BF16)
    solved[0] = value
    earlier = value
    for row in range(1, rows):
        base = dot(inverse[row], rhs[row]) - dot(folded[row, :, width:], earlier)
        if row + 1 < rows:
            earlier = solved[cols[row + 1, 1]]
        value = (base - dot(folded[row, :, :width], value)).astype(BF16)
        solved[row] = value
    copies[3].wait()
    copies[4].wait()
    for level in range(sep_blocks.shape[0]):
        pair = jnp.concatenate([sep_blocks[level, 0], sep_blocks[level, 1]], axis=1)
        sources = jnp.concatenate(
            [solved[sep_cols[level, 0]], solved[sep_cols[level, 1]]], axis=0
        )
        total = dot(pair, sources)
        partial[level] = total - jnp.where(own_level[0] == level, sep_rhs[...].astype(F32), 0.0)


def path_kernel(core, partial, mine, other, low, high):
    for level in range(partial.shape[0]):
        total = partial[level]
        if 1 <= level <= LOW:
            total = total - dot(whole(core, mine, other, level - 1), value)
        value = total.astype(BF16)
        if level < LOW:
            low[level] = value.T
        else:
            spread_out(high, level - LOW, value)


def plane_kernel(core, arrived, mine, other, fourth, above):
    sources = arrived.shape[0]
    value = sum(arrived[source, 0].astype(F32) for source in range(sources)).astype(BF16)
    fourth[...] = value
    for index in range(above.shape[1]):
        total = sum(arrived[source, index + 1].astype(F32) for source in range(sources))
        value = (total - dot_nt(value, whole(core, mine, other, index))).astype(BF16)
        for piece in range(above.shape[0]):
            above[piece, index] = value


def top_kernel(core, place, arrived, fourth, mine, other, spread):
    planes = arrived.shape[0]
    for level in range(spread.shape[1]):
        if level == 0:
            total = fourth[...]
        else:
            index = level - 1
            total = jnp.zeros(fourth.shape, F32)
            for source in range(planes):
                share = arrived[source, index].astype(F32)
                if 2 << index < planes:
                    near = (place[0] >> (index + 1)) == (source >> (index + 1))
                    share = jnp.where(near, share, 0.0)
                total = total + share
            total = total.astype(BF16)
        value = -dot(total, whole(core, mine, other, level))
        value = value.astype(BF16)
        for piece in range(spread.shape[0]):
            spread[piece, level] = value


def prepare_kernel(cols, sep_cols, solved, inverse, lower, sep_blocks, start, chain, couple):
    rows = solved.shape[0]
    for row in range(rows):
        start[row] = dot_t(inverse[row], solved[row])
    for row in range(1, rows):
        for slot in range(2):
            column = cols[row, slot] if slot else row - 1
            chain[row, slot] = dot(lower[row, slot], inverse[column]).astype(BF16).T
    for level in range(sep_blocks.shape[0]):
        for slot in range(2):
            product = dot(sep_blocks[level, slot], inverse[sep_cols[level, slot]])
            couple[level, slot] = product.astype(BF16).T


def backward_kernel(cols, sep_cols, core, own_level, *refs):
    far, (solution, own), near, (pending, nodes, sems) = (
        refs[:13],
        refs[13:15],
        refs[15:-3],
        refs[-3:],
    )
    far = far[:7] + tuple(stack.at[0] for stack in far[7:10]) + far[10:]
    copies = start_all(far, near, sems)
    high, gains_high, gains_high_other, gains_low, gains_low_other = near[:5]
    finish, finish_other = near[5:7]
    low = near[7:10]
    couple, start, chain = near[10:]
    rows = start.shape[0]
    count = nodes.shape[0]
    split = gains_low.shape[0]
    for copy in copies[:10]:
        copy.wait()
    for level in range(count - 1, -1, -1):
        if level < LOW:
            node = -dot(low[level][...], whole(core, finish, finish_other, level))
        else:
            pieces = [high[piece, level - LOW] for piece in range(high.shape[0])]
            node = jnp.concatenate(pieces, axis=0).astype(F32)
        if level + 1 < count:
            if level < split:
                gain = whole(core, gains_low, gains_low_other, level)
            else:
                gain = whole(core, gains_high, gains_high_other, level - split)
            node = node - dot(vector, gain)
        vector = node.astype(BF16)
        nodes[level] = vector
    own[...] = nodes[own_level[0]].T
    for copy in copies[10:]:
        copy.wait()
    pending[...] = start[...]
    for level in range(count - 1, -1, -1):
        for slot in range(2):
            column = sep_cols[level, slot]
            pending[column] = pending[column] - dot_nt(couple[level, slot], nodes[level])
    following = pending[rows - 1]
    for row in range(rows - 1, -1, -1):
        value = following.astype(BF16)
        solution[row] = value
        if row:
            following = pending[row - 1] - dot(chain[row, 0], value)
            if row > 1:
                column = cols[row, 1]
                pending[column] = pending[column] - dot(chain[row, 1], value)
            else:
                following = following - dot(chain[row, 1], value)


def other_core(mine):
    cores = lax.axis_size("cols")
    return lax.ppermute(mine, "cols", [(i, cores - 1 - i) for i in range(cores)])


def with_other_core(flags, pairs):
    mine = jnp.stack([jnp.where(flags[i] == 1, *pair[::-1]) for i, pair in enumerate(pairs)])
    return mine, other_core(mine)


def after(value, earlier):
    return lax.optimization_barrier((value, earlier))[0]


def per_device(
    rhs,
    diag_inverse,
    lower_blocks,
    local_cols,
    sep_rhs,
    sep_blocks,
    sep_cols,
    sep_inverse,
    sep_link,
):
    size = lax.axis_size("blk")
    device = lax.axis_index("blk")
    cores = lax.axis_size("cols")
    bits = size.bit_length() - 1
    count = bits + 1
    rows, width, columns = rhs.shape
    sep_width = sep_rhs.shape[1]
    plane = 1 << PLANE_BITS
    slice_rows = columns // plane
    sep_cols = sep_cols[0]
    sep_blocks = sep_blocks[0]
    own_level = sum(
        (((device + 1) & (2**k - 1)) == 0).astype(jnp.int32) for k in range(1, count)
    )[None]

    def step_mask(bit):
        base = 0 if bit < 2 else 2 if bit < 4 else 4
        return (2 << bit) - (1 << base)

    core = lax.axis_index("cols")[None]
    half = shaped((sep_width // cores, sep_width), BF16)
    gain, finish = in_vmem(
        gain_kernel,
        [half, half],
        [core],
        [sep_inverse[0], sep_link[0]],
        [pltpu.VMEM((2, sep_width, sep_width), BF16)],
    )

    flags = (device >> jnp.arange(count, dtype=jnp.int32)) & 1

    def climb(top, bit):
        mask = step_mask(bit)
        arrived = lax.ppermute(top, "blk", [(i, i ^ mask) for i in range(size)])
        return (top, arrived), jnp.where(flags[bit] == 1, top, arrived)

    piece = (slice_rows, sep_width)
    groups = [[g * plane + i for i in range(plane)] for g in range(size // plane)]
    towers = [[g + i * plane for i in range(size // plane)] for g in range(plane)]

    def within(value, members):
        return lax.all_to_all(value, "blk", 0, 0, axis_index_groups=members, tiled=True)

    arrays = [diag_inverse, lower_blocks, after(rhs, gain), sep_blocks, sep_rhs[0]]
    solved, partial = placed(
        forward_kernel,
        [shaped(rhs.shape, BF16), shaped((count, sep_width, columns), F32)],
        [local_cols, sep_cols, own_level],
        arrays,
        [pltpu.VMEM(array.shape, array.dtype) for array in arrays]
        + [pltpu.VMEM((rows, width, 2 * width), BF16), pltpu.SemaphoreType.DMA((len(arrays),))],
    )
    gain_list, finish_list = [], []

    def climb_gain(bit):
        nonlocal gain
        pair, gain = climb(gain, bit)
        gain_list.append(pair)

    def climb_finish(bit):
        nonlocal finish
        pair, finish = climb(finish, bit)
        finish_list.append(pair)

    def both(bit, event=None):
        nonlocal gain, finish
        finish = after(finish, gain)
        if event is not None:
            gain, finish = after(gain, event), after(finish, event)
        climb_gain(bit)
        climb_finish(bit - 1)

    climb_gain(0)
    both(1, solved)
    for bit in range(2, LOW):
        both(bit)
    gains_low = with_other_core(flags[:LOW], gain_list)
    both(LOW)
    both(LOW + 1)
    low, shares = in_vmem(
        path_kernel,
        [shaped((LOW, columns, sep_width), BF16), shaped((plane, count - LOW, *piece), BF16)],
        [core],
        [partial, *gains_low],
    )
    both(LOW + 2, shares)
    arrived = within(shares, groups)

    def added(mine, other):
        return (mine.astype(F32) + other.astype(F32)).astype(BF16)

    def swapped(value, bit):
        mask = step_mask(bit)
        return added(value, lax.ppermute(value, "blk", [(i, i ^ mask) for i in range(size)]))

    low1 = swapped(after(low, arrived), 0)
    both(LOW + 3, arrived)
    gains_high = with_other_core(flags[LOW:bits], gain_list[LOW:])
    climb_finish(bits - 1)
    finish_list.append((finish, finish))
    fourth, above = in_vmem(
        plane_kernel,
        [shaped(piece, BF16), shaped((size // plane, bits - LOW, *piece), BF16)],
        [core],
        [arrived, *gains_high],
    )
    finish_high = with_other_core(flags[LOW:], finish_list[LOW:])
    low2 = swapped(after(low1[1:], above), 1)
    arrived = after(within(above, towers), low2)
    (spread,) = in_vmem(
        top_kernel,
        [shaped((plane, count - LOW, *piece), BF16)],
        [core, (device >> PLANE_BITS)[None]],
        [arrived, fourth, *finish_high],
    )
    low3 = swapped(after(low2[1:], spread), 2)
    finish_low = with_other_core(flags[:LOW], finish_list[:LOW])
    start, chain, couple = in_vmem(
        prepare_kernel,
        [
            shaped(rhs.shape, F32),
            shaped((rows, 2, width, width), BF16),
            shaped((count, 2, width, sep_width), BF16),
        ],
        [local_cols, sep_cols],
        [after(solved, spread), diag_inverse, lower_blocks, sep_blocks],
    )
    high = within(spread, groups)
    far = [high, *gains_high, *gains_low, *finish_low, low1, low2, low3, couple, start, chain]
    shapes = [array.shape[1:] if 7 <= i < 10 else array.shape for i, array in enumerate(far)]
    solution, own = placed(
        backward_kernel,
        [shaped(rhs.shape, BF16), shaped((sep_width, columns), BF16)],
        [local_cols, sep_cols, core, own_level],
        far,
        [pltpu.VMEM(shape, array.dtype) for shape, array in zip(shapes, far)]
        + [
            pltpu.VMEM(rhs.shape, F32),
            pltpu.VMEM((count, columns, sep_width), BF16),
            pltpu.SemaphoreType.DMA((len(far),)),
        ],
    )
    return solution, own[None]


def solution(mesh):
    return jax.shard_map(
        per_device,
        mesh=mesh,
        in_specs=(
            P("blk", None, "cols"),
            P("blk", None, None),
            P("blk", None, None, None),
            P("blk", None),
            P("blk", None, "cols"),
            P("blk", None, None, None, None),
            P("blk", None, None),
            P("blk", None, None),
            P("blk", None, None),
        ),
        out_specs=(P("blk", None, "cols"), P("blk", None, "cols")),
        check_vma=False,
    )
```

```python
import jax
import jax.numpy as jnp
from jax import lax
from jax.experimental import pallas as pl
from jax.experimental.pallas import tpu as pltpu
from jax.sharding import PartitionSpec as P

F32 = jnp.float32
BF16 = jnp.bfloat16
PLANE_BITS = 4
LOW = 3


def dot(left, right):
    return jnp.dot(left, right, preferred_element_type=F32)


def dot_t(left, right):
    return lax.dot_general(left, right, (((0,), (0,)), ((), ())), preferred_element_type=F32)


def dot_nt(left, right):
    return lax.dot_general(left, right, (((1,), (1,)), ((), ())), preferred_element_type=F32)


def start_all(far, near, sems):
    copies = [pltpu.make_async_copy(far[i], near[i], sems.at[i]) for i in range(len(far))]
    for copy in copies:
        copy.start()
    return copies


def in_vmem(kernel, outs, scalars, arrays, scratch=()):
    counts = len(scalars), len(arrays), len(outs), len(arrays)

    def loaded(*refs):
        parts, first = [], 0
        for amount in counts:
            parts.append(refs[first : first + amount])
            first += amount
        small, far, results, near = parts
        for copy in start_all(far, near, refs[-1]):
            copy.wait()
        kernel(*small, *near, *results, *refs[first:-1])

    return placed(
        loaded,
        outs,
        scalars,
        arrays,
        [pltpu.VMEM(array.shape, array.dtype) for array in arrays]
        + list(scratch)
        + [pltpu.SemaphoreType.DMA((len(arrays),))],
    )


def placed(kernel, outs, scalars, arrays, scratch):
    vmem, smem = pl.BlockSpec(memory_space=pltpu.VMEM), pl.BlockSpec(memory_space=pltpu.SMEM)
    moved = sum(a.size * a.dtype.itemsize for a in arrays)
    moved += sum(o.size * o.dtype.itemsize for o in outs)
    return pl.pallas_call(
        kernel,
        out_shape=tuple(outs),
        in_specs=[smem] * len(scalars) + [pl.BlockSpec(memory_space=pl.ANY)] * len(arrays),
        out_specs=tuple(vmem for _ in outs),
        scratch_shapes=scratch,
        compiler_params=pltpu.CompilerParams(vmem_limit_bytes=56 * 2**20),
        cost_estimate=pl.CostEstimate(flops=10**9, bytes_accessed=moved, transcendentals=0),
    )(*scalars, *arrays)


def shaped(shape, dtype):
    return jax.ShapeDtypeStruct(shape, dtype)


def whole(core, mine, other, index):
    if mine.shape[1] == mine.shape[2]:
        return mine[index]
    first = core[0] == 0
    upper = jnp.where(first, mine[index], other[index])
    lower = jnp.where(first, other[index], mine[index])
    return jnp.concatenate([upper, lower], axis=0)


def gain_kernel(core, inverse, link, gain, finish, full):
    own = inverse[...]
    full[0] = dot(link[...], own).astype(BF16)
    full[1] = dot_t(own, own).astype(BF16)
    rows = gain.shape[0]
    first = pl.multiple_of(core[0] * rows, rows)
    gain[...] = full[0, pl.ds(first, rows)]
    finish[...] = full[1, pl.ds(first, rows)]


def spread_out(pieces, index, value):
    turned = value.T
    rows = pieces.shape[2]
    for piece in range(pieces.shape[0]):
        pieces[piece, index] = turned[piece * rows : (piece + 1) * rows]


def solve_rows(cols, first, inverse, lower, rhs, solved, folded, arrive):
    rows, width, _ = rhs.shape
    arrive(0)
    for row in range(rows):
        if first + row:
            pair = jnp.concatenate([lower[row, 0], lower[row, 1]], axis=1)
            folded[row] = dot(inverse[row], pair).astype(BF16)
    arrive(1)
    for row in range(rows):
        base = dot(inverse[row], rhs[row])
        if first + row:
            if row == 0:
                value = solved[first - 1]
                earlier = solved[cols[first, 1]]
            elif first + row == 1:
                earlier = value
            base = base - dot(folded[row, :, width:], earlier)
            base = base - dot(folded[row, :, :width], value)
        if row + 1 < rows and first + row:
            earlier = solved[cols[first + row + 1, 1]]
        value = base.astype(BF16)
        solved[first + row] = value


def first_kernel(cols, *refs):
    far, (solved,), near, (folded, sems) = refs[:3], refs[3:4], refs[4:7], refs[7:]
    rows = solved.shape[0]
    inverse, lower, rhs = near
    copies = start_all([ref.at[pl.ds(0, rows)] for ref in far], near, sems)

    def arrive(stage):
        for copy in copies[2:] if stage else copies[:2]:
            copy.wait()

    solve_rows(cols, 0, inverse, lower, rhs, solved, folded, arrive)


def second_kernel(cols, sep_cols, own_level, *refs):
    far, (solved, partial), near, (folded, sems) = refs[:6], refs[6:8], refs[8:13], refs[13:]
    inverse, lower, rhs, sep_blocks, sep_rhs = near
    rows = rhs.shape[0]
    views = [ref.at[pl.ds(rows, rows)] for ref in far[:3]] + list(far[3:5])
    copies = start_all(views + [far[5]], [*near, solved.at[pl.ds(0, rows)]], sems)

    def arrive(stage):
        for copy in (copies[2], copies[5]) if stage else copies[:2]:
            copy.wait()

    solve_rows(cols, rows, inverse, lower, rhs, solved, folded, arrive)
    copies[3].wait()
    copies[4].wait()
    for level in range(sep_blocks.shape[0]):
        pair = jnp.concatenate([sep_blocks[level, 0], sep_blocks[level, 1]], axis=1)
        sources = jnp.concatenate(
            [solved[sep_cols[level, 0]], solved[sep_cols[level, 1]]], axis=0
        )
        total = dot(pair, sources)
        partial[level] = total - jnp.where(own_level[0] == level, sep_rhs[...].astype(F32), 0.0)


def path_kernel(core, partial, mine, other, low, high):
    for level in range(partial.shape[0]):
        total = partial[level]
        if 1 <= level <= LOW:
            total = total - dot(whole(core, mine, other, level - 1), value)
        value = total.astype(BF16)
        if level < LOW:
            low[level] = value.T
        else:
            spread_out(high, level - LOW, value)


def plane_kernel(core, arrived, mine, other, fourth, above):
    sources = arrived.shape[0]
    value = sum(arrived[source, 0].astype(F32) for source in range(sources)).astype(BF16)
    fourth[...] = value
    for index in range(above.shape[1]):
        total = sum(arrived[source, index + 1].astype(F32) for source in range(sources))
        value = (total - dot_nt(value, whole(core, mine, other, index))).astype(BF16)
        for piece in range(above.shape[0]):
            above[piece, index] = value


def top_kernel(core, place, arrived, fourth, mine, other, spread):
    planes = arrived.shape[0]
    for level in range(spread.shape[1]):
        if level == 0:
            total = fourth[...]
        else:
            index = level - 1
            total = jnp.zeros(fourth.shape, F32)
            for source in range(planes):
                share = arrived[source, index].astype(F32)
                if 2 << index < planes:
                    near = (place[0] >> (index + 1)) == (source >> (index + 1))
                    share = jnp.where(near, share, 0.0)
                total = total + share
            total = total.astype(BF16)
        value = -dot(total, whole(core, mine, other, level))
        value = value.astype(BF16)
        for piece in range(spread.shape[0]):
            spread[piece, level] = value


def prepare_kernel(cols, sep_cols, solved, inverse, lower, sep_blocks, start, chain, couple):
    rows = solved.shape[0]
    for row in range(rows):
        start[row] = dot_t(inverse[row], solved[row])
    for row in range(1, rows):
        for slot in range(2):
            column = cols[row, slot] if slot else row - 1
            chain[row, slot] = dot(lower[row, slot], inverse[column]).astype(BF16).T
    for level in range(sep_blocks.shape[0]):
        for slot in range(2):
            product = dot(sep_blocks[level, slot], inverse[sep_cols[level, slot]])
            couple[level, slot] = product.astype(BF16).T


def backward_kernel(cols, sep_cols, core, own_level, *refs):
    far, (solution, own), near, (pending, nodes, sems) = (
        refs[:13],
        refs[13:15],
        refs[15:-3],
        refs[-3:],
    )
    far = far[:7] + tuple(stack.at[0] for stack in far[7:10]) + far[10:]
    copies = start_all(far, near, sems)
    high, gains_high, gains_high_other, gains_low, gains_low_other = near[:5]
    finish, finish_other = near[5:7]
    low = near[7:10]
    couple, start, chain = near[10:]
    rows = start.shape[0]
    count = nodes.shape[0]
    split = gains_low.shape[0]
    for copy in copies[:10]:
        copy.wait()
    for level in range(count - 1, -1, -1):
        if level < LOW:
            node = -dot(low[level][...], whole(core, finish, finish_other, level))
        else:
            pieces = [high[piece, level - LOW] for piece in range(high.shape[0])]
            node = jnp.concatenate(pieces, axis=0).astype(F32)
        if level + 1 < count:
            if level < split:
                gain = whole(core, gains_low, gains_low_other, level)
            else:
                gain = whole(core, gains_high, gains_high_other, level - split)
            node = node - dot(vector, gain)
        vector = node.astype(BF16)
        nodes[level] = vector
    own[...] = nodes[own_level[0]].T
    for copy in copies[10:]:
        copy.wait()
    pending[...] = start[...]
    for level in range(count - 1, -1, -1):
        for slot in range(2):
            column = sep_cols[level, slot]
            pending[column] = pending[column] - dot_nt(couple[level, slot], nodes[level])
    following = pending[rows - 1]
    for row in range(rows - 1, -1, -1):
        value = following.astype(BF16)
        solution[row] = value
        if row:
            following = pending[row - 1] - dot(chain[row, 0], value)
            if row > 1:
                column = cols[row, 1]
                pending[column] = pending[column] - dot(chain[row, 1], value)
            else:
                following = following - dot(chain[row, 1], value)


def other_core(mine):
    cores = lax.axis_size("cols")
    return lax.ppermute(mine, "cols", [(i, cores - 1 - i) for i in range(cores)])


def with_other_core(flags, pairs):
    mine = jnp.stack([jnp.where(flags[i] == 1, *pair[::-1]) for i, pair in enumerate(pairs)])
    return mine, other_core(mine)


def after(value, earlier):
    return lax.optimization_barrier((value, earlier))[0]


def per_device(
    rhs,
    diag_inverse,
    lower_blocks,
    local_cols,
    sep_rhs,
    sep_blocks,
    sep_cols,
    sep_inverse,
    sep_link,
):
    size = lax.axis_size("blk")
    device = lax.axis_index("blk")
    cores = lax.axis_size("cols")
    bits = size.bit_length() - 1
    count = bits + 1
    rows, width, columns = rhs.shape
    sep_width = sep_rhs.shape[1]
    plane = 1 << PLANE_BITS
    slice_rows = columns // plane
    sep_cols = sep_cols[0]
    sep_blocks = sep_blocks[0]
    own_level = sum(
        (((device + 1) & (2**k - 1)) == 0).astype(jnp.int32) for k in range(1, count)
    )[None]

    def step_mask(bit):
        base = 0 if bit < 2 else 2 if bit < 4 else 4
        return (2 << bit) - (1 << base)

    core = lax.axis_index("cols")[None]
    half = shaped((sep_width // cores, sep_width), BF16)
    gain, finish = in_vmem(
        gain_kernel,
        [half, half],
        [core],
        [sep_inverse[0], sep_link[0]],
        [pltpu.VMEM((2, sep_width, sep_width), BF16)],
    )

    flags = (device >> jnp.arange(count, dtype=jnp.int32)) & 1

    def climb(top, bit):
        mask = step_mask(bit)
        arrived = lax.ppermute(top, "blk", [(i, i ^ mask) for i in range(size)])
        return (top, arrived), jnp.where(flags[bit] == 1, top, arrived)

    piece = (slice_rows, sep_width)
    groups = [[g * plane + i for i in range(plane)] for g in range(size // plane)]
    towers = [[g + i * plane for i in range(size // plane)] for g in range(plane)]

    def within(value, members):
        return lax.all_to_all(value, "blk", 0, 0, axis_index_groups=members, tiled=True)

    half_rows = rows // 2
    halves = [
        pltpu.VMEM((half_rows, *array.shape[1:]), BF16)
        for array in (diag_inverse, lower_blocks, rhs)
    ]
    folded = pltpu.VMEM((half_rows, width, 2 * width), BF16)
    (solved_first,) = placed(
        first_kernel,
        [shaped((half_rows, width, columns), BF16)],
        [local_cols],
        [diag_inverse, lower_blocks, after(rhs, gain)],
        [*halves, folded, pltpu.SemaphoreType.DMA((3,))],
    )
    solved, partial = placed(
        second_kernel,
        [shaped(rhs.shape, BF16), shaped((count, sep_width, columns), F32)],
        [local_cols, sep_cols, own_level],
        [diag_inverse, lower_blocks, rhs, sep_blocks, sep_rhs[0], solved_first],
        [
            *halves,
            pltpu.VMEM(sep_blocks.shape, BF16),
            pltpu.VMEM(sep_rhs.shape[1:], BF16),
            folded,
            pltpu.SemaphoreType.DMA((6,)),
        ],
    )
    gain_list, finish_list = [], []

    def climb_gain(bit):
        nonlocal gain
        pair, gain = climb(gain, bit)
        gain_list.append(pair)

    def climb_finish(bit):
        nonlocal finish
        pair, finish = climb(finish, bit)
        finish_list.append(pair)

    def both(bit):
        nonlocal finish
        finish = after(finish, gain)
        climb_gain(bit)
        climb_finish(bit - 2)

    climb_gain(0)
    gain = after(gain, solved_first)
    climb_gain(1)
    both(2)
    gains_low = with_other_core(flags[:LOW], gain_list)
    both(LOW)
    low, shares = in_vmem(
        path_kernel,
        [shaped((LOW, columns, sep_width), BF16), shaped((plane, count - LOW, *piece), BF16)],
        [core],
        [partial, *gains_low],
    )
    arrived = within(shares, groups)
    gain = after(gain, shares)
    both(LOW + 1)
    both(LOW + 2)
    both(LOW + 3)

    def added(mine, other):
        return (mine.astype(F32) + other.astype(F32)).astype(BF16)

    def swapped(value, bit):
        mask = step_mask(bit)
        return added(value, lax.ppermute(value, "blk", [(i, i ^ mask) for i in range(size)]))

    low1 = swapped(after(low, arrived), 0)
    gain_list[-1] = after(gain_list[-1], arrived)
    gains_high = with_other_core(flags[LOW:bits], gain_list[LOW:])
    finish = after(finish, gain)
    climb_finish(bits - 2)
    fourth, above = in_vmem(
        plane_kernel,
        [shaped(piece, BF16), shaped((size // plane, bits - LOW, *piece), BF16)],
        [core],
        [arrived, *gains_high],
    )
    finish = after(after(finish, above), low1)
    climb_finish(bits - 1)
    finish_list.append((finish, finish))
    finish_high = with_other_core(flags[LOW:], finish_list[LOW:])
    low2 = swapped(low1[1:], 1)
    low3 = swapped(low2[1:], 2)
    arrived = after(within(above, towers), low3)
    (spread,) = in_vmem(
        top_kernel,
        [shaped((plane, count - LOW, *piece), BF16)],
        [core, (device >> PLANE_BITS)[None]],
        [arrived, fourth, *finish_high],
    )
    finish_low = with_other_core(flags[:LOW], finish_list[:LOW])
    start, chain, couple = in_vmem(
        prepare_kernel,
        [
            shaped(rhs.shape, F32),
            shaped((rows, 2, width, width), BF16),
            shaped((count, 2, width, sep_width), BF16),
        ],
        [local_cols, sep_cols],
        [after(solved, spread), diag_inverse, lower_blocks, sep_blocks],
    )
    high = within(spread, groups)
    far = [high, *gains_high, *gains_low, *finish_low, low1, low2, low3, couple, start, chain]
    shapes = [array.shape[1:] if 7 <= i < 10 else array.shape for i, array in enumerate(far)]
    solution, own = placed(
        backward_kernel,
        [shaped(rhs.shape, BF16), shaped((sep_width, columns), BF16)],
        [local_cols, sep_cols, core, own_level],
        far,
        [pltpu.VMEM(shape, array.dtype) for shape, array in zip(shapes, far)]
        + [
            pltpu.VMEM(rhs.shape, F32),
            pltpu.VMEM((count, columns, sep_width), BF16),
            pltpu.SemaphoreType.DMA((len(far),)),
        ],
    )
    return solution, own[None]


def solution(mesh):
    return jax.shard_map(
        per_device,
        mesh=mesh,
        in_specs=(
            P("blk", None, "cols"),
            P("blk", None, None),
            P("blk", None, None, None),
            P("blk", None),
            P("blk", None, "cols"),
            P("blk", None, None, None, None),
            P("blk", None, None),
            P("blk", None, None),
            P("blk", None, None),
        ),
        out_specs=(P("blk", None, "cols"), P("blk", None, "cols")),
        check_vma=False,
    )
```

```python
import jax
import jax.numpy as jnp
from jax import lax
from jax.experimental import pallas as pl
from jax.experimental.pallas import tpu as pltpu
from jax.sharding import PartitionSpec as P

F32 = jnp.float32
BF16 = jnp.bfloat16
PLANE_BITS = 4
LOW = 3


def dot(left, right):
    return jnp.dot(left, right, preferred_element_type=F32)


def dot_t(left, right):
    return lax.dot_general(left, right, (((0,), (0,)), ((), ())), preferred_element_type=F32)


def dot_nt(left, right):
    return lax.dot_general(left, right, (((1,), (1,)), ((), ())), preferred_element_type=F32)


def start_all(far, near, sems):
    copies = [pltpu.make_async_copy(far[i], near[i], sems.at[i]) for i in range(len(far))]
    for copy in copies:
        copy.start()
    return copies


def start_picked(flags, pairs, near, sems):
    for index, (first, second) in enumerate(pairs):

        @pl.when(flags[index] == 0)
        def _():
            pltpu.make_async_copy(first, near.at[index], sems.at[index]).start()

        @pl.when(flags[index] != 0)
        def _():
            pltpu.make_async_copy(second, near.at[index], sems.at[index]).start()

    return [
        pltpu.make_async_copy(pair[0], near.at[index], sems.at[index])
        for index, pair in enumerate(pairs)
    ]


def in_vmem(kernel, outs, scalars, arrays, scratch=()):
    counts = len(scalars), len(arrays), len(outs), len(arrays)

    def loaded(*refs):
        parts, first = [], 0
        for amount in counts:
            parts.append(refs[first : first + amount])
            first += amount
        small, far, results, near = parts
        for copy in start_all(far, near, refs[-1]):
            copy.wait()
        kernel(*small, *near, *results, *refs[first:-1])

    return placed(
        loaded,
        outs,
        scalars,
        arrays,
        [pltpu.VMEM(array.shape, array.dtype) for array in arrays]
        + list(scratch)
        + [pltpu.SemaphoreType.DMA((len(arrays),))],
    )


def placed(kernel, outs, scalars, arrays, scratch):
    vmem, smem = pl.BlockSpec(memory_space=pltpu.VMEM), pl.BlockSpec(memory_space=pltpu.SMEM)
    moved = sum(a.size * a.dtype.itemsize for a in arrays)
    moved += sum(o.size * o.dtype.itemsize for o in outs)
    return pl.pallas_call(
        kernel,
        out_shape=tuple(outs),
        in_specs=[smem] * len(scalars) + [pl.BlockSpec(memory_space=pl.ANY)] * len(arrays),
        out_specs=tuple(vmem for _ in outs),
        scratch_shapes=scratch,
        compiler_params=pltpu.CompilerParams(vmem_limit_bytes=56 * 2**20),
        cost_estimate=pl.CostEstimate(flops=10**9, bytes_accessed=moved, transcendentals=0),
    )(*scalars, *arrays)


def shaped(shape, dtype):
    return jax.ShapeDtypeStruct(shape, dtype)


def whole(core, mine, other, index):
    if mine.shape[1] == mine.shape[2]:
        return mine[index]
    first = core[0] == 0
    upper = jnp.where(first, mine[index], other[index])
    lower = jnp.where(first, other[index], mine[index])
    return jnp.concatenate([upper, lower], axis=0)


def gain_kernel(core, inverse, link, gain, finish, full):
    own = inverse[...]
    full[...] = dot(link[...], own).astype(BF16)
    rows = gain.shape[0]
    gain[...] = full[pl.ds(pl.multiple_of(core[0] * rows, rows), rows)]
    finish[...] = dot_t(own, own).astype(BF16)


def spread_out(pieces, index, value):
    turned = value.T
    rows = pieces.shape[2]
    for piece in range(pieces.shape[0]):
        pieces[piece, index] = turned[piece * rows : (piece + 1) * rows]


def solve_rows(cols, first, inverse, lower, rhs, solved, folded, arrive):
    rows, width, _ = rhs.shape
    arrive(0)
    for row in range(rows):
        if first + row:
            pair = jnp.concatenate([lower[row, 0], lower[row, 1]], axis=1)
            folded[row] = dot(inverse[row], pair).astype(BF16)
    arrive(1)
    for row in range(rows):
        base = dot(inverse[row], rhs[row])
        if first + row:
            if row == 0:
                value = solved[first - 1]
                earlier = solved[cols[first, 1]]
            elif first + row == 1:
                earlier = value
            base = base - dot(folded[row, :, width:], earlier)
            base = base - dot(folded[row, :, :width], value)
        if row + 1 < rows and first + row:
            earlier = solved[cols[first + row + 1, 1]]
        value = base.astype(BF16)
        solved[first + row] = value


def first_kernel(cols, *refs):
    far, (solved,), near, (folded, sems) = refs[:3], refs[3:4], refs[4:7], refs[7:]
    rows = solved.shape[0]
    inverse, lower, rhs = near
    copies = start_all([ref.at[pl.ds(0, rows)] for ref in far], near, sems)

    def arrive(stage):
        for copy in copies[2:] if stage else copies[:2]:
            copy.wait()

    solve_rows(cols, 0, inverse, lower, rhs, solved, folded, arrive)


def second_kernel(cols, sep_cols, own_level, *refs):
    far, (solved, partial), near, (folded, sems) = refs[:6], refs[6:8], refs[8:13], refs[13:]
    inverse, lower, rhs, sep_blocks, sep_rhs = near
    rows = rhs.shape[0]
    views = [ref.at[pl.ds(rows, rows)] for ref in far[:3]] + list(far[3:5])
    copies = start_all(views + [far[5]], [*near, solved.at[pl.ds(0, rows)]], sems)

    def arrive(stage):
        for copy in (copies[2], copies[5]) if stage else copies[:2]:
            copy.wait()

    solve_rows(cols, rows, inverse, lower, rhs, solved, folded, arrive)
    copies[3].wait()
    copies[4].wait()
    for level in range(sep_blocks.shape[0]):
        pair = jnp.concatenate([sep_blocks[level, 0], sep_blocks[level, 1]], axis=1)
        sources = jnp.concatenate(
            [solved[sep_cols[level, 0]], solved[sep_cols[level, 1]]], axis=0
        )
        total = dot(pair, sources)
        partial[level] = total - jnp.where(own_level[0] == level, sep_rhs[...].astype(F32), 0.0)


def path_kernel(core, partial, mine, other, low, high):
    for level in range(partial.shape[0]):
        total = partial[level]
        if 1 <= level <= LOW:
            total = total - dot(whole(core, mine, other, level - 1), value)
        value = total.astype(BF16)
        if level < LOW:
            low[level] = value.T
        else:
            spread_out(high, level - LOW, value)


def plane_kernel(core, arrived, mine, other, fourth, above):
    sources = arrived.shape[0]
    value = sum(arrived[source, 0].astype(F32) for source in range(sources)).astype(BF16)
    fourth[...] = value
    for index in range(above.shape[1]):
        total = sum(arrived[source, index + 1].astype(F32) for source in range(sources))
        value = (total - dot_nt(value, whole(core, mine, other, index))).astype(BF16)
        for piece in range(above.shape[0]):
            above[piece, index] = value


def top_kernel(place, flags, *refs):
    far, spread, (arrived, fourth, finish, sems) = refs[:-5], refs[-5], refs[-4:]
    copies = start_all(far[:2], (arrived, fourth), sems)
    pairs = list(zip(far[2::2], far[3::2]))
    copies += start_picked(flags, pairs, finish, sems.at[pl.ds(2, len(pairs))])
    for copy in copies:
        copy.wait()
    planes = arrived.shape[0]
    for level in range(spread.shape[1]):
        if level == 0:
            total = fourth[...]
        else:
            index = level - 1
            total = jnp.zeros(fourth.shape, F32)
            for source in range(planes):
                share = arrived[source, index].astype(F32)
                if 2 << index < planes:
                    near = (place[0] >> (index + 1)) == (source >> (index + 1))
                    share = jnp.where(near, share, 0.0)
                total = total + share
            total = total.astype(BF16)
        value = -dot(total, finish[level])
        value = value.astype(BF16)
        for piece in range(spread.shape[0]):
            spread[piece, level] = value


def prepare_kernel(cols, sep_cols, solved, inverse, lower, sep_blocks, start, chain, couple):
    rows = solved.shape[0]
    for row in range(rows):
        start[row] = dot_t(inverse[row], solved[row])
    for row in range(1, rows):
        for slot in range(2):
            column = cols[row, slot] if slot else row - 1
            chain[row, slot] = dot(lower[row, slot], inverse[column]).astype(BF16).T
    for level in range(sep_blocks.shape[0]):
        for slot in range(2):
            product = dot(sep_blocks[level, slot], inverse[sep_cols[level, slot]])
            couple[level, slot] = product.astype(BF16).T


def backward_kernel(cols, sep_cols, core, own_level, flags, *refs):
    far, (solution, own), near, (finish, pending, nodes, sems) = (
        refs[:17],
        refs[17:19],
        refs[19:-4],
        refs[-4:],
    )
    direct = far[:5] + tuple(stack.at[0] for stack in far[5:8]) + far[8:11]
    copies = start_all(direct[:8], near[:8], sems)
    pairs = list(zip(far[11::2], far[12::2]))
    copies += start_picked(flags, pairs, finish, sems.at[pl.ds(11, LOW)])
    later = start_all(direct[8:], near[8:], sems.at[pl.ds(8, 3)])
    high, gains_high, gains_high_other, gains_low, gains_low_other = near[:5]
    low = near[5:8]
    couple, start, chain = near[8:]
    rows = start.shape[0]
    count = nodes.shape[0]
    split = gains_low.shape[0]
    for copy in copies:
        copy.wait()
    for level in range(count - 1, -1, -1):
        if level < LOW:
            node = -dot(low[level][...], finish[level])
        else:
            pieces = [high[piece, level - LOW] for piece in range(high.shape[0])]
            node = jnp.concatenate(pieces, axis=0).astype(F32)
        if level + 1 < count:
            if level < split:
                gain = whole(core, gains_low, gains_low_other, level)
            else:
                gain = whole(core, gains_high, gains_high_other, level - split)
            node = node - dot(vector, gain)
        vector = node.astype(BF16)
        nodes[level] = vector
    own[...] = nodes[own_level[0]].T
    for copy in later:
        copy.wait()
    pending[...] = start[...]
    for level in range(count - 1, -1, -1):
        for slot in range(2):
            column = sep_cols[level, slot]
            pending[column] = pending[column] - dot_nt(couple[level, slot], nodes[level])
    following = pending[rows - 1]
    for row in range(rows - 1, -1, -1):
        value = following.astype(BF16)
        solution[row] = value
        if row:
            following = pending[row - 1] - dot(chain[row, 0], value)
            if row > 1:
                column = cols[row, 1]
                pending[column] = pending[column] - dot(chain[row, 1], value)
            else:
                following = following - dot(chain[row, 1], value)


def other_core(mine):
    cores = lax.axis_size("cols")
    return lax.ppermute(mine, "cols", [(i, cores - 1 - i) for i in range(cores)])


def with_other_core(flags, pairs):
    mine = jnp.stack([jnp.where(flags[i] == 1, *pair[::-1]) for i, pair in enumerate(pairs)])
    return mine, other_core(mine)


def after(value, earlier):
    return lax.optimization_barrier((value, earlier))[0]


def per_device(
    rhs,
    diag_inverse,
    lower_blocks,
    local_cols,
    sep_rhs,
    sep_blocks,
    sep_cols,
    sep_inverse,
    sep_link,
):
    size = lax.axis_size("blk")
    device = lax.axis_index("blk")
    cores = lax.axis_size("cols")
    bits = size.bit_length() - 1
    count = bits + 1
    rows, width, columns = rhs.shape
    sep_width = sep_rhs.shape[1]
    plane = 1 << PLANE_BITS
    slice_rows = columns // plane
    sep_cols = sep_cols[0]
    sep_blocks = sep_blocks[0]
    own_level = sum(
        (((device + 1) & (2**k - 1)) == 0).astype(jnp.int32) for k in range(1, count)
    )[None]

    def step_mask(bit):
        base = 0 if bit < 2 else 2 if bit < 4 else 4
        return (2 << bit) - (1 << base)

    core = lax.axis_index("cols")[None]
    gain, finish = in_vmem(
        gain_kernel,
        [shaped((sep_width // cores, sep_width), BF16), shaped((sep_width, sep_width), BF16)],
        [core],
        [sep_inverse[0], sep_link[0]],
        [pltpu.VMEM((sep_width, sep_width), BF16)],
    )

    flags = (device >> jnp.arange(count, dtype=jnp.int32)) & 1

    def climb(top, bit):
        mask = step_mask(bit)
        arrived = lax.ppermute(top, "blk", [(i, i ^ mask) for i in range(size)])
        return (top, arrived), jnp.where(flags[bit] == 1, top, arrived)

    piece = (slice_rows, sep_width)
    groups = [[g * plane + i for i in range(plane)] for g in range(size // plane)]
    towers = [[g + i * plane for i in range(size // plane)] for g in range(plane)]

    def within(value, members):
        return lax.all_to_all(value, "blk", 0, 0, axis_index_groups=members, tiled=True)

    half_rows = rows // 2
    halves = [
        pltpu.VMEM((half_rows, *array.shape[1:]), BF16)
        for array in (diag_inverse, lower_blocks, rhs)
    ]
    folded = pltpu.VMEM((half_rows, width, 2 * width), BF16)
    (solved_first,) = placed(
        first_kernel,
        [shaped((half_rows, width, columns), BF16)],
        [local_cols],
        [diag_inverse, lower_blocks, after(rhs, gain)],
        [*halves, folded, pltpu.SemaphoreType.DMA((3,))],
    )
    solved, partial = placed(
        second_kernel,
        [shaped(rhs.shape, BF16), shaped((count, sep_width, columns), F32)],
        [local_cols, sep_cols, own_level],
        [diag_inverse, lower_blocks, rhs, sep_blocks, sep_rhs[0], solved_first],
        [
            *halves,
            pltpu.VMEM(sep_blocks.shape, BF16),
            pltpu.VMEM(sep_rhs.shape[1:], BF16),
            folded,
            pltpu.SemaphoreType.DMA((6,)),
        ],
    )
    gain_list, finish_list = [], []

    def climb_gain(bit):
        nonlocal gain
        pair, gain = climb(gain, bit)
        gain_list.append(pair)

    def climb_finish(bit):
        nonlocal finish
        pair, finish = climb(finish, bit)
        finish_list.append(pair)

    def both(bit):
        nonlocal finish
        finish = after(finish, gain)
        climb_gain(bit)
        climb_finish(bit - 1)

    climb_gain(0)
    gain = after(gain, solved_first)
    both(1)
    both(2)
    gains_low = with_other_core(flags[:LOW], gain_list)
    both(LOW)
    low, shares = in_vmem(
        path_kernel,
        [shaped((LOW, columns, sep_width), BF16), shaped((plane, count - LOW, *piece), BF16)],
        [core],
        [partial, *gains_low],
    )
    arrived = within(shares, groups)
    gain = after(gain, shares)
    both(LOW + 1)
    both(LOW + 2)
    both(LOW + 3)

    def added(mine, other):
        return (mine.astype(F32) + other.astype(F32)).astype(BF16)

    def swapped(value, bit):
        mask = step_mask(bit)
        return added(value, lax.ppermute(value, "blk", [(i, i ^ mask) for i in range(size)]))

    low1 = swapped(low, 0)
    low2 = swapped(low1[1:], 1)
    low3 = swapped(low2[1:], 2)
    gain_list[-1] = after(gain_list[-1], arrived)
    gains_high = with_other_core(flags[LOW:bits], gain_list[LOW:])
    finish = after(finish, gain)
    climb_finish(bits - 1)
    finish_list.append((finish, finish))
    fourth, above = in_vmem(
        plane_kernel,
        [shaped(piece, BF16), shaped((size // plane, bits - LOW, *piece), BF16)],
        [core],
        [after(arrived, (low3, finish)), *gains_high],
    )
    arrived = within(above, towers)
    matrix = (sep_width, sep_width)
    (spread,) = placed(
        top_kernel,
        [shaped((plane, count - LOW, *piece), BF16)],
        [(device >> PLANE_BITS)[None], flags[LOW:]],
        [arrived, fourth, *[array for pair in finish_list[LOW:] for array in pair]],
        [
            pltpu.VMEM(arrived.shape, BF16),
            pltpu.VMEM(piece, BF16),
            pltpu.VMEM((count - LOW, *matrix), BF16),
            pltpu.SemaphoreType.DMA((2 + count - LOW,)),
        ],
    )
    start, chain, couple = in_vmem(
        prepare_kernel,
        [
            shaped(rhs.shape, F32),
            shaped((rows, 2, width, width), BF16),
            shaped((count, 2, width, sep_width), BF16),
        ],
        [local_cols, sep_cols],
        [after(solved, spread), diag_inverse, lower_blocks, sep_blocks],
    )
    high = within(spread, groups)
    far = [high, *gains_high, *gains_low, low1, low2, low3, couple, start, chain]
    shapes = [array.shape[1:] if 5 <= i < 8 else array.shape for i, array in enumerate(far)]
    solution, own = placed(
        backward_kernel,
        [shaped(rhs.shape, BF16), shaped((sep_width, columns), BF16)],
        [local_cols, sep_cols, core, own_level, flags],
        far + [array for pair in finish_list[:LOW] for array in pair],
        [pltpu.VMEM(shape, array.dtype) for shape, array in zip(shapes, far)]
        + [
            pltpu.VMEM((LOW, *matrix), BF16),
            pltpu.VMEM(rhs.shape, F32),
            pltpu.VMEM((count, columns, sep_width), BF16),
            pltpu.SemaphoreType.DMA((len(far) + LOW,)),
        ],
    )
    return solution, own[None]


def solution(mesh):
    return jax.shard_map(
        per_device,
        mesh=mesh,
        in_specs=(
            P("blk", None, "cols"),
            P("blk", None, None),
            P("blk", None, None, None),
            P("blk", None),
            P("blk", None, "cols"),
            P("blk", None, None, None, None),
            P("blk", None, None),
            P("blk", None, None),
            P("blk", None, None),
        ),
        out_specs=(P("blk", None, "cols"), P("blk", None, "cols")),
        check_vma=False,
    )
```

```python
import jax
import jax.numpy as jnp
from jax import lax
from jax.experimental import pallas as pl
from jax.experimental.pallas import tpu as pltpu
from jax.sharding import PartitionSpec as P

F32 = jnp.float32
BF16 = jnp.bfloat16
PLANE_BITS = 4
LOW = 3


def dot(left, right):
    return jnp.dot(left, right, preferred_element_type=F32)


def dot_t(left, right):
    return lax.dot_general(left, right, (((0,), (0,)), ((), ())), preferred_element_type=F32)


def dot_nt(left, right):
    return lax.dot_general(left, right, (((1,), (1,)), ((), ())), preferred_element_type=F32)


def start_all(far, near, sems):
    copies = [pltpu.make_async_copy(far[i], near[i], sems.at[i]) for i in range(len(far))]
    for copy in copies:
        copy.start()
    return copies


def in_vmem(kernel, outs, scalars, arrays, scratch=()):
    counts = len(scalars), len(arrays), len(outs), len(arrays)

    def loaded(*refs):
        parts, first = [], 0
        for amount in counts:
            parts.append(refs[first : first + amount])
            first += amount
        small, far, results, near = parts
        for copy in start_all(far, near, refs[-1]):
            copy.wait()
        kernel(*small, *near, *results, *refs[first:-1])

    return placed(
        loaded,
        outs,
        scalars,
        arrays,
        [pltpu.VMEM(array.shape, array.dtype) for array in arrays]
        + list(scratch)
        + [pltpu.SemaphoreType.DMA((len(arrays),))],
    )


def placed(kernel, outs, scalars, arrays, scratch):
    vmem, smem = pl.BlockSpec(memory_space=pltpu.VMEM), pl.BlockSpec(memory_space=pltpu.SMEM)
    moved = sum(a.size * a.dtype.itemsize for a in arrays)
    moved += sum(o.size * o.dtype.itemsize for o in outs)
    return pl.pallas_call(
        kernel,
        out_shape=tuple(outs),
        in_specs=[smem] * len(scalars) + [pl.BlockSpec(memory_space=pl.ANY)] * len(arrays),
        out_specs=tuple(vmem for _ in outs),
        scratch_shapes=scratch,
        compiler_params=pltpu.CompilerParams(vmem_limit_bytes=56 * 2**20),
        cost_estimate=pl.CostEstimate(flops=10**9, bytes_accessed=moved, transcendentals=0),
    )(*scalars, *arrays)


def shaped(shape, dtype):
    return jax.ShapeDtypeStruct(shape, dtype)


def whole(core, mine, other, index):
    if mine.shape[1] == mine.shape[2]:
        return mine[index]
    first = core[0] == 0
    upper = jnp.where(first, mine[index], other[index])
    lower = jnp.where(first, other[index], mine[index])
    return jnp.concatenate([upper, lower], axis=0)


def gain_kernel(core, inverse, link, gain, finish, full):
    own = inverse[...]
    full[0] = dot(link[...], own).astype(BF16)
    full[1] = dot_t(own, own).astype(BF16)
    rows = gain.shape[0]
    first = pl.multiple_of(core[0] * rows, rows)
    gain[...] = full[0, pl.ds(first, rows)]
    finish[...] = full[1, pl.ds(first, rows)]


def spread_out(pieces, index, value):
    turned = value.T
    rows = pieces.shape[2]
    for piece in range(pieces.shape[0]):
        pieces[piece, index] = turned[piece * rows : (piece + 1) * rows]


def solve_rows(cols, first, inverse, lower, rhs, solved, folded, arrive):
    rows, width, _ = rhs.shape
    arrive(0)
    for row in range(rows):
        if first + row:
            pair = jnp.concatenate([lower[row, 0], lower[row, 1]], axis=1)
            folded[row] = dot(inverse[row], pair).astype(BF16)
    arrive(1)
    for row in range(rows):
        base = dot(inverse[row], rhs[row])
        if first + row:
            if row == 0:
                value = solved[first - 1]
                earlier = solved[cols[first, 1]]
            elif first + row == 1:
                earlier = value
            base = base - dot(folded[row, :, width:], earlier)
            base = base - dot(folded[row, :, :width], value)
        if row + 1 < rows and first + row:
            earlier = solved[cols[first + row + 1, 1]]
        value = base.astype(BF16)
        solved[first + row] = value


def first_kernel(cols, *refs):
    far, (solved,), near, (folded, sems) = refs[:3], refs[3:4], refs[4:7], refs[7:]
    rows = solved.shape[0]
    inverse, lower, rhs = near
    copies = start_all([ref.at[pl.ds(0, rows)] for ref in far], near, sems)

    def arrive(stage):
        for copy in copies[2:] if stage else copies[:2]:
            copy.wait()

    solve_rows(cols, 0, inverse, lower, rhs, solved, folded, arrive)


def second_kernel(cols, sep_cols, own_level, *refs):
    far, (solved, partial), near, (folded, sems) = refs[:6], refs[6:8], refs[8:13], refs[13:]
    inverse, lower, rhs, sep_blocks, sep_rhs = near
    rows = rhs.shape[0]
    views = [ref.at[pl.ds(rows, rows)] for ref in far[:3]] + list(far[3:5])
    copies = start_all(views + [far[5]], [*near, solved.at[pl.ds(0, rows)]], sems)

    def arrive(stage):
        for copy in (copies[2], copies[5]) if stage else copies[:2]:
            copy.wait()

    solve_rows(cols, rows, inverse, lower, rhs, solved, folded, arrive)
    copies[3].wait()
    copies[4].wait()
    for level in range(sep_blocks.shape[0]):
        pair = jnp.concatenate([sep_blocks[level, 0], sep_blocks[level, 1]], axis=1)
        sources = jnp.concatenate(
            [solved[sep_cols[level, 0]], solved[sep_cols[level, 1]]], axis=0
        )
        total = dot(pair, sources)
        partial[level] = total - jnp.where(own_level[0] == level, sep_rhs[...].astype(F32), 0.0)


def path_kernel(core, partial, mine, other, low, high):
    for level in range(partial.shape[0]):
        total = partial[level]
        if 1 <= level <= LOW:
            total = total - dot(whole(core, mine, other, level - 1), value)
        value = total.astype(BF16)
        if level < LOW:
            low[level] = value.T
        else:
            spread_out(high, level - LOW, value)


def plane_kernel(core, arrived, mine, other, fourth, above):
    sources = arrived.shape[0]
    value = sum(arrived[source, 0].astype(F32) for source in range(sources)).astype(BF16)
    fourth[...] = value
    for index in range(above.shape[1]):
        total = sum(arrived[source, index + 1].astype(F32) for source in range(sources))
        value = (total - dot_nt(value, whole(core, mine, other, index))).astype(BF16)
        for piece in range(above.shape[0]):
            above[piece, index] = value


def top_kernel(core, place, arrived, fourth, mine, other, spread):
    planes = arrived.shape[0]
    for level in range(spread.shape[1]):
        if level == 0:
            total = fourth[...]
        else:
            index = level - 1
            total = jnp.zeros(fourth.shape, F32)
            for source in range(planes):
                share = arrived[source, index].astype(F32)
                if 2 << index < planes:
                    near = (place[0] >> (index + 1)) == (source >> (index + 1))
                    share = jnp.where(near, share, 0.0)
                total = total + share
            total = total.astype(BF16)
        value = -dot(total, whole(core, mine, other, level))
        value = value.astype(BF16)
        for piece in range(spread.shape[0]):
            spread[piece, level] = value


def prepare_kernel(cols, sep_cols, solved, inverse, lower, sep_blocks, start, chain, couple):
    rows = solved.shape[0]
    for row in range(rows):
        start[row] = dot_t(inverse[row], solved[row])
    for row in range(1, rows):
        for slot in range(2):
            column = cols[row, slot] if slot else row - 1
            chain[row, slot] = dot(lower[row, slot], inverse[column]).astype(BF16).T
    for level in range(sep_blocks.shape[0]):
        for slot in range(2):
            product = dot(sep_blocks[level, slot], inverse[sep_cols[level, slot]])
            couple[level, slot] = product.astype(BF16).T


def backward_kernel(cols, sep_cols, core, own_level, *refs):
    far, (solution, own), near, (pending, nodes, sems) = (
        refs[:13],
        refs[13:15],
        refs[15:-3],
        refs[-3:],
    )
    far = far[:7] + tuple(stack.at[0] for stack in far[7:10]) + far[10:]
    copies = start_all(far, near, sems)
    high, gains_high, gains_high_other, gains_low, gains_low_other = near[:5]
    finish, finish_other = near[5:7]
    low = near[7:10]
    couple, start, chain = near[10:]
    rows = start.shape[0]
    count = nodes.shape[0]
    split = gains_low.shape[0]
    for copy in copies[:10]:
        copy.wait()
    for level in range(count - 1, -1, -1):
        if level < LOW:
            node = -dot(low[level][...], whole(core, finish, finish_other, level))
        else:
            pieces = [high[piece, level - LOW] for piece in range(high.shape[0])]
            node = jnp.concatenate(pieces, axis=0).astype(F32)
        if level + 1 < count:
            if level < split:
                gain = whole(core, gains_low, gains_low_other, level)
            else:
                gain = whole(core, gains_high, gains_high_other, level - split)
            node = node - dot(vector, gain)
        vector = node.astype(BF16)
        nodes[level] = vector
    own[...] = nodes[own_level[0]].T
    for copy in copies[10:]:
        copy.wait()
    pending[...] = start[...]
    for level in range(count - 1, -1, -1):
        for slot in range(2):
            column = sep_cols[level, slot]
            pending[column] = pending[column] - dot_nt(couple[level, slot], nodes[level])
    following = pending[rows - 1]
    for row in range(rows - 1, -1, -1):
        value = following.astype(BF16)
        solution[row] = value
        if row:
            following = pending[row - 1] - dot(chain[row, 0], value)
            if row > 1:
                column = cols[row, 1]
                pending[column] = pending[column] - dot(chain[row, 1], value)
            else:
                following = following - dot(chain[row, 1], value)


def other_core(mine):
    cores = lax.axis_size("cols")
    return lax.ppermute(mine, "cols", [(i, cores - 1 - i) for i in range(cores)])


def with_other_core(flags, pairs):
    mine = jnp.stack([jnp.where(flags[i] == 1, *pair[::-1]) for i, pair in enumerate(pairs)])
    return mine, other_core(mine)


def after(value, earlier):
    return lax.optimization_barrier((value, earlier))[0]


def per_device(
    rhs,
    diag_inverse,
    lower_blocks,
    local_cols,
    sep_rhs,
    sep_blocks,
    sep_cols,
    sep_inverse,
    sep_link,
):
    size = lax.axis_size("blk")
    device = lax.axis_index("blk")
    cores = lax.axis_size("cols")
    bits = size.bit_length() - 1
    count = bits + 1
    rows, width, columns = rhs.shape
    sep_width = sep_rhs.shape[1]
    plane = 1 << PLANE_BITS
    slice_rows = columns // plane
    sep_cols = sep_cols[0]
    sep_blocks = sep_blocks[0]
    own_level = sum(
        (((device + 1) & (2**k - 1)) == 0).astype(jnp.int32) for k in range(1, count)
    )[None]

    def step_mask(bit):
        base = 0 if bit < 2 else 2 if bit < 4 else 4
        return (2 << bit) - (1 << base)

    core = lax.axis_index("cols")[None]
    half = shaped((sep_width // cores, sep_width), BF16)
    gain, finish = in_vmem(
        gain_kernel,
        [half, half],
        [core],
        [sep_inverse[0], sep_link[0]],
        [pltpu.VMEM((2, sep_width, sep_width), BF16)],
    )

    flags = (device >> jnp.arange(count, dtype=jnp.int32)) & 1

    def climb(top, bit):
        mask = step_mask(bit)
        arrived = lax.ppermute(top, "blk", [(i, i ^ mask) for i in range(size)])
        return (top, arrived), jnp.where(flags[bit] == 1, top, arrived)

    piece = (slice_rows, sep_width)
    groups = [[g * plane + i for i in range(plane)] for g in range(size // plane)]
    towers = [[g + i * plane for i in range(size // plane)] for g in range(plane)]

    def within(value, members):
        return lax.all_to_all(value, "blk", 0, 0, axis_index_groups=members, tiled=True)

    half_rows = rows // 2
    halves = [
        pltpu.VMEM((half_rows, *array.shape[1:]), BF16)
        for array in (diag_inverse, lower_blocks, rhs)
    ]
    folded = pltpu.VMEM((half_rows, width, 2 * width), BF16)
    (solved_first,) = placed(
        first_kernel,
        [shaped((half_rows, width, columns), BF16)],
        [local_cols],
        [diag_inverse, lower_blocks, after(rhs, gain)],
        [*halves, folded, pltpu.SemaphoreType.DMA((3,))],
    )
    solved, partial = placed(
        second_kernel,
        [shaped(rhs.shape, BF16), shaped((count, sep_width, columns), F32)],
        [local_cols, sep_cols, own_level],
        [diag_inverse, lower_blocks, rhs, sep_blocks, sep_rhs[0], solved_first],
        [
            *halves,
            pltpu.VMEM(sep_blocks.shape, BF16),
            pltpu.VMEM(sep_rhs.shape[1:], BF16),
            folded,
            pltpu.SemaphoreType.DMA((6,)),
        ],
    )
    gain_list, finish_list = [], []

    def climb_gain(bit):
        nonlocal gain
        pair, gain = climb(gain, bit)
        gain_list.append(pair)

    def climb_finish(bit):
        nonlocal finish
        pair, finish = climb(finish, bit)
        finish_list.append(pair)

    def both(bit, event=None):
        nonlocal gain, finish
        finish = after(finish, gain)
        if event is not None:
            gain, finish = after(gain, event), after(finish, event)
        climb_gain(bit)
        climb_finish(bit - 1)

    climb_gain(0)
    both(1, solved_first)
    for bit in range(2, LOW):
        both(bit)
    gains_low = with_other_core(flags[:LOW], gain_list)
    both(LOW)
    both(LOW + 1)
    low, shares = in_vmem(
        path_kernel,
        [shaped((LOW, columns, sep_width), BF16), shaped((plane, count - LOW, *piece), BF16)],
        [core],
        [partial, *gains_low],
    )
    both(LOW + 2, shares)
    arrived = within(shares, groups)

    def added(mine, other):
        return (mine.astype(F32) + other.astype(F32)).astype(BF16)

    def swapped(value, bit):
        mask = step_mask(bit)
        return added(value, lax.ppermute(value, "blk", [(i, i ^ mask) for i in range(size)]))

    low1 = swapped(after(low, arrived), 0)
    both(LOW + 3, arrived)
    gains_high = with_other_core(flags[LOW:bits], gain_list[LOW:])
    climb_finish(bits - 1)
    finish_list.append((finish, finish))
    fourth, above = in_vmem(
        plane_kernel,
        [shaped(piece, BF16), shaped((size // plane, bits - LOW, *piece), BF16)],
        [core],
        [after(arrived, low1), *gains_high],
    )
    finish_high = with_other_core(flags[LOW:], finish_list[LOW:])
    low2 = swapped(low1[1:], 1)
    low3 = swapped(low2[1:], 2)
    arrived = after(within(above, towers), low3)
    (spread,) = in_vmem(
        top_kernel,
        [shaped((plane, count - LOW, *piece), BF16)],
        [core, (device >> PLANE_BITS)[None]],
        [arrived, fourth, *finish_high],
    )
    finish_low = with_other_core(flags[:LOW], finish_list[:LOW])
    start, chain, couple = in_vmem(
        prepare_kernel,
        [
            shaped(rhs.shape, F32),
            shaped((rows, 2, width, width), BF16),
            shaped((count, 2, width, sep_width), BF16),
        ],
        [local_cols, sep_cols],
        [after(solved, spread), diag_inverse, lower_blocks, sep_blocks],
    )
    high = within(spread, groups)
    far = [high, *gains_high, *gains_low, *finish_low, low1, low2, low3, couple, start, chain]
    shapes = [array.shape[1:] if 7 <= i < 10 else array.shape for i, array in enumerate(far)]
    solution, own = placed(
        backward_kernel,
        [shaped(rhs.shape, BF16), shaped((sep_width, columns), BF16)],
        [local_cols, sep_cols, core, own_level],
        far,
        [pltpu.VMEM(shape, array.dtype) for shape, array in zip(shapes, far)]
        + [
            pltpu.VMEM(rhs.shape, F32),
            pltpu.VMEM((count, columns, sep_width), BF16),
            pltpu.SemaphoreType.DMA((len(far),)),
        ],
    )
    return solution, own[None]


def solution(mesh):
    return jax.shard_map(
        per_device,
        mesh=mesh,
        in_specs=(
            P("blk", None, "cols"),
            P("blk", None, None),
            P("blk", None, None, None),
            P("blk", None),
            P("blk", None, "cols"),
            P("blk", None, None, None, None),
            P("blk", None, None),
            P("blk", None, None),
            P("blk", None, None),
        ),
        out_specs=(P("blk", None, "cols"), P("blk", None, "cols")),
        check_vma=False,
    )
```

```python
import jax
import jax.numpy as jnp
from jax import lax
from jax.experimental import pallas as pl
from jax.experimental.pallas import tpu as pltpu
from jax.sharding import PartitionSpec as P

F32 = jnp.float32
BF16 = jnp.bfloat16
PLANE_BITS = 4
LOW = 3


def dot(left, right):
    return jnp.dot(left, right, preferred_element_type=F32)


def dot_t(left, right):
    return lax.dot_general(left, right, (((0,), (0,)), ((), ())), preferred_element_type=F32)


def dot_nt(left, right):
    return lax.dot_general(left, right, (((1,), (1,)), ((), ())), preferred_element_type=F32)


def start_all(far, near, sems):
    copies = [pltpu.make_async_copy(far[i], near[i], sems.at[i]) for i in range(len(far))]
    for copy in copies:
        copy.start()
    return copies


def in_vmem(kernel, outs, scalars, arrays, scratch=()):
    counts = len(scalars), len(arrays), len(outs), len(arrays)

    def loaded(*refs):
        parts, first = [], 0
        for amount in counts:
            parts.append(refs[first : first + amount])
            first += amount
        small, far, results, near = parts
        for copy in start_all(far, near, refs[-1]):
            copy.wait()
        kernel(*small, *near, *results, *refs[first:-1])

    return placed(
        loaded,
        outs,
        scalars,
        arrays,
        [pltpu.VMEM(array.shape, array.dtype) for array in arrays]
        + list(scratch)
        + [pltpu.SemaphoreType.DMA((len(arrays),))],
    )


def placed(kernel, outs, scalars, arrays, scratch):
    vmem, smem = pl.BlockSpec(memory_space=pltpu.VMEM), pl.BlockSpec(memory_space=pltpu.SMEM)
    moved = sum(a.size * a.dtype.itemsize for a in arrays)
    moved += sum(o.size * o.dtype.itemsize for o in outs)
    return pl.pallas_call(
        kernel,
        out_shape=tuple(outs),
        in_specs=[smem] * len(scalars) + [pl.BlockSpec(memory_space=pl.ANY)] * len(arrays),
        out_specs=tuple(vmem for _ in outs),
        scratch_shapes=scratch,
        compiler_params=pltpu.CompilerParams(vmem_limit_bytes=56 * 2**20),
        cost_estimate=pl.CostEstimate(flops=10**9, bytes_accessed=moved, transcendentals=0),
    )(*scalars, *arrays)


def shaped(shape, dtype):
    return jax.ShapeDtypeStruct(shape, dtype)


def whole(core, mine, other, index):
    if mine.shape[1] == mine.shape[2]:
        return mine[index]
    first = core[0] == 0
    upper = jnp.where(first, mine[index], other[index])
    lower = jnp.where(first, other[index], mine[index])
    return jnp.concatenate([upper, lower], axis=0)


def gain_kernel(core, inverse, link, gain, finish, full):
    own = inverse[...]
    full[0] = dot(link[...], own).astype(BF16)
    full[1] = dot_t(own, own).astype(BF16)
    rows = gain.shape[0]
    first = pl.multiple_of(core[0] * rows, rows)
    gain[...] = full[0, pl.ds(first, rows)]
    finish[...] = full[1, pl.ds(first, rows)]


def spread_out(pieces, index, value):
    turned = value.T
    rows = pieces.shape[2]
    for piece in range(pieces.shape[0]):
        pieces[piece, index] = turned[piece * rows : (piece + 1) * rows]


def solve_rows(cols, first, inverse, lower, rhs, solved, folded, arrive):
    rows, width, _ = rhs.shape
    arrive(0)
    for row in range(rows):
        if first + row:
            pair = jnp.concatenate([lower[row, 0], lower[row, 1]], axis=1)
            folded[row] = dot(inverse[row], pair).astype(BF16)
    arrive(1)
    for row in range(rows):
        base = dot(inverse[row], rhs[row])
        if first + row:
            if row == 0:
                value = solved[first - 1]
                earlier = solved[cols[first, 1]]
            elif first + row == 1:
                earlier = value
            base = base - dot(folded[row, :, width:], earlier)
            base = base - dot(folded[row, :, :width], value)
        if row + 1 < rows and first + row:
            earlier = solved[cols[first + row + 1, 1]]
        value = base.astype(BF16)
        solved[first + row] = value


def first_kernel(cols, *refs):
    far, (solved,), near, (folded, sems) = refs[:3], refs[3:4], refs[4:7], refs[7:]
    rows = solved.shape[0]
    inverse, lower, rhs = near
    copies = start_all([ref.at[pl.ds(0, rows)] for ref in far], near, sems)

    def arrive(stage):
        for copy in copies[2:] if stage else copies[:2]:
            copy.wait()

    solve_rows(cols, 0, inverse, lower, rhs, solved, folded, arrive)


def second_kernel(cols, sep_cols, own_level, *refs):
    far, (solved, partial), near, (folded, sems) = refs[:6], refs[6:8], refs[8:13], refs[13:]
    inverse, lower, rhs, sep_blocks, sep_rhs = near
    rows = rhs.shape[0]
    views = [ref.at[pl.ds(rows, rows)] for ref in far[:3]] + list(far[3:5])
    copies = start_all(views + [far[5]], [*near, solved.at[pl.ds(0, rows)]], sems)

    def arrive(stage):
        for copy in (copies[2], copies[5]) if stage else copies[:2]:
            copy.wait()

    solve_rows(cols, rows, inverse, lower, rhs, solved, folded, arrive)
    copies[3].wait()
    copies[4].wait()
    for level in range(sep_blocks.shape[0]):
        pair = jnp.concatenate([sep_blocks[level, 0], sep_blocks[level, 1]], axis=1)
        sources = jnp.concatenate(
            [solved[sep_cols[level, 0]], solved[sep_cols[level, 1]]], axis=0
        )
        total = dot(pair, sources)
        partial[level] = total - jnp.where(own_level[0] == level, sep_rhs[...].astype(F32), 0.0)


def path_kernel(core, partial, mine, other, low, high):
    for level in range(partial.shape[0]):
        total = partial[level]
        if 1 <= level <= LOW:
            total = total - dot(whole(core, mine, other, level - 1), value)
        value = total.astype(BF16)
        if level < LOW:
            low[level] = value.T
        else:
            spread_out(high, level - LOW, value)


def plane_kernel(core, arrived, mine, other, fourth, above):
    sources = arrived.shape[0]
    value = sum(arrived[source, 0].astype(F32) for source in range(sources)).astype(BF16)
    fourth[...] = value
    for index in range(above.shape[1]):
        total = sum(arrived[source, index + 1].astype(F32) for source in range(sources))
        value = (total - dot_nt(value, whole(core, mine, other, index))).astype(BF16)
        for piece in range(above.shape[0]):
            above[piece, index] = value


def top_kernel(core, place, arrived, fourth, mine, other, spread):
    planes = arrived.shape[0]
    for level in range(spread.shape[1]):
        if level == 0:
            total = fourth[...]
        else:
            index = level - 1
            total = jnp.zeros(fourth.shape, F32)
            for source in range(planes):
                share = arrived[source, index].astype(F32)
                if 2 << index < planes:
                    near = (place[0] >> (index + 1)) == (source >> (index + 1))
                    share = jnp.where(near, share, 0.0)
                total = total + share
            total = total.astype(BF16)
        value = -dot(total, whole(core, mine, other, level))
        value = value.astype(BF16)
        for piece in range(spread.shape[0]):
            spread[piece, level] = value


def prepare_kernel(cols, sep_cols, solved, inverse, lower, sep_blocks, start, chain, couple):
    rows = solved.shape[0]
    for row in range(rows):
        start[row] = dot_t(inverse[row], solved[row])
    for row in range(1, rows):
        for slot in range(2):
            column = cols[row, slot] if slot else row - 1
            chain[row, slot] = dot(lower[row, slot], inverse[column]).astype(BF16).T
    for level in range(sep_blocks.shape[0]):
        for slot in range(2):
            product = dot(sep_blocks[level, slot], inverse[sep_cols[level, slot]])
            couple[level, slot] = product.astype(BF16).T


def backward_kernel(cols, sep_cols, core, own_level, *refs):
    far, (solution, own), near, (pending, nodes, sems) = (
        refs[:13],
        refs[13:15],
        refs[15:-3],
        refs[-3:],
    )
    far = far[:7] + tuple(stack.at[0] for stack in far[7:10]) + far[10:]
    copies = start_all(far, near, sems)
    high, gains_high, gains_high_other, gains_low, gains_low_other = near[:5]
    finish, finish_other = near[5:7]
    low = near[7:10]
    couple, start, chain = near[10:]
    rows = start.shape[0]
    count = nodes.shape[0]
    split = gains_low.shape[0]
    for copy in copies[:10]:
        copy.wait()
    for level in range(count - 1, -1, -1):
        if level < LOW:
            node = -dot(low[level][...], whole(core, finish, finish_other, level))
        else:
            pieces = [high[piece, level - LOW] for piece in range(high.shape[0])]
            node = jnp.concatenate(pieces, axis=0).astype(F32)
        if level + 1 < count:
            if level < split:
                gain = whole(core, gains_low, gains_low_other, level)
            else:
                gain = whole(core, gains_high, gains_high_other, level - split)
            node = node - dot(vector, gain)
        vector = node.astype(BF16)
        nodes[level] = vector
    own[...] = nodes[own_level[0]].T
    for copy in copies[10:]:
        copy.wait()
    pending[...] = start[...]
    for level in range(count - 1, -1, -1):
        for slot in range(2):
            column = sep_cols[level, slot]
            pending[column] = pending[column] - dot_nt(couple[level, slot], nodes[level])
    following = pending[rows - 1]
    for row in range(rows - 1, -1, -1):
        value = following.astype(BF16)
        solution[row] = value
        if row:
            following = pending[row - 1] - dot(chain[row, 0], value)
            if row > 1:
                column = cols[row, 1]
                pending[column] = pending[column] - dot(chain[row, 1], value)
            else:
                following = following - dot(chain[row, 1], value)


def other_core(mine):
    cores = lax.axis_size("cols")
    return lax.ppermute(mine, "cols", [(i, cores - 1 - i) for i in range(cores)])


def with_other_core(flags, pairs):
    mine = jnp.stack([jnp.where(flags[i] == 1, *pair[::-1]) for i, pair in enumerate(pairs)])
    return mine, other_core(mine)


def after(value, earlier):
    return lax.optimization_barrier((value, earlier))[0]


def per_device(
    rhs,
    diag_inverse,
    lower_blocks,
    local_cols,
    sep_rhs,
    sep_blocks,
    sep_cols,
    sep_inverse,
    sep_link,
):
    size = lax.axis_size("blk")
    device = lax.axis_index("blk")
    cores = lax.axis_size("cols")
    bits = size.bit_length() - 1
    count = bits + 1
    rows, width, columns = rhs.shape
    sep_width = sep_rhs.shape[1]
    plane = 1 << PLANE_BITS
    slice_rows = columns // plane
    sep_cols = sep_cols[0]
    sep_blocks = sep_blocks[0]
    own_level = sum(
        (((device + 1) & (2**k - 1)) == 0).astype(jnp.int32) for k in range(1, count)
    )[None]

    def step_mask(bit):
        base = 0 if bit < 2 else 2 if bit < 4 else 4
        return (2 << bit) - (1 << base)

    core = lax.axis_index("cols")[None]
    half = shaped((sep_width // cores, sep_width), BF16)
    gain, finish = in_vmem(
        gain_kernel,
        [half, half],
        [core],
        [sep_inverse[0], sep_link[0]],
        [pltpu.VMEM((2, sep_width, sep_width), BF16)],
    )

    flags = (device >> jnp.arange(count, dtype=jnp.int32)) & 1

    def climb(top, bit):
        mask = step_mask(bit)
        arrived = lax.ppermute(top, "blk", [(i, i ^ mask) for i in range(size)])
        return (top, arrived), jnp.where(flags[bit] == 1, top, arrived)

    piece = (slice_rows, sep_width)
    groups = [[g * plane + i for i in range(plane)] for g in range(size // plane)]
    towers = [[g + i * plane for i in range(size // plane)] for g in range(plane)]

    def within(value, members):
        return lax.all_to_all(value, "blk", 0, 0, axis_index_groups=members, tiled=True)

    half_rows = rows // 2
    halves = [
        pltpu.VMEM((half_rows, *array.shape[1:]), BF16)
        for array in (diag_inverse, lower_blocks, rhs)
    ]
    folded = pltpu.VMEM((half_rows, width, 2 * width), BF16)
    (solved_first,) = placed(
        first_kernel,
        [shaped((half_rows, width, columns), BF16)],
        [local_cols],
        [diag_inverse, lower_blocks, after(rhs, gain)],
        [*halves, folded, pltpu.SemaphoreType.DMA((3,))],
    )
    solved, partial = placed(
        second_kernel,
        [shaped(rhs.shape, BF16), shaped((count, sep_width, columns), F32)],
        [local_cols, sep_cols, own_level],
        [diag_inverse, lower_blocks, rhs, sep_blocks, sep_rhs[0], solved_first],
        [
            *halves,
            pltpu.VMEM(sep_blocks.shape, BF16),
            pltpu.VMEM(sep_rhs.shape[1:], BF16),
            folded,
            pltpu.SemaphoreType.DMA((6,)),
        ],
    )
    gain_list, finish_list = [], []

    def climb_gain(bit):
        nonlocal gain
        pair, gain = climb(gain, bit)
        gain_list.append(pair)

    def climb_finish(bit):
        nonlocal finish
        pair, finish = climb(finish, bit)
        finish_list.append(pair)

    def both(bit, event=None):
        nonlocal gain, finish
        finish = after(finish, gain)
        if event is not None:
            gain, finish = after(gain, event), after(finish, event)
        climb_gain(bit)
        climb_finish(bit - 1)

    climb_gain(0)
    both(1, solved_first)
    for bit in range(2, LOW):
        both(bit, solved)
    gains_low = with_other_core(flags[:LOW], gain_list)
    both(LOW)
    both(LOW + 1)
    low, shares = in_vmem(
        path_kernel,
        [shaped((LOW, columns, sep_width), BF16), shaped((plane, count - LOW, *piece), BF16)],
        [core],
        [partial, *gains_low],
    )
    both(LOW + 2, shares)
    arrived = within(shares, groups)

    def added(mine, other):
        return (mine.astype(F32) + other.astype(F32)).astype(BF16)

    def swapped(value, bit):
        mask = step_mask(bit)
        return added(value, lax.ppermute(value, "blk", [(i, i ^ mask) for i in range(size)]))

    low1 = swapped(after(low, arrived), 0)
    both(LOW + 3, arrived)
    gains_high = with_other_core(flags[LOW:bits], gain_list[LOW:])
    climb_finish(bits - 1)
    finish_list.append((finish, finish))
    fourth, above = in_vmem(
        plane_kernel,
        [shaped(piece, BF16), shaped((size // plane, bits - LOW, *piece), BF16)],
        [core],
        [after(arrived, low1), *gains_high],
    )
    finish_high = with_other_core(flags[LOW:], finish_list[LOW:])
    low2 = swapped(low1[1:], 1)
    low3 = swapped(low2[1:], 2)
    arrived = after(within(above, towers), low3)
    (spread,) = in_vmem(
        top_kernel,
        [shaped((plane, count - LOW, *piece), BF16)],
        [core, (device >> PLANE_BITS)[None]],
        [arrived, fourth, *finish_high],
    )
    finish_low = with_other_core(flags[:LOW], finish_list[:LOW])
    start, chain, couple = in_vmem(
        prepare_kernel,
        [
            shaped(rhs.shape, F32),
            shaped((rows, 2, width, width), BF16),
            shaped((count, 2, width, sep_width), BF16),
        ],
        [local_cols, sep_cols],
        [after(solved, spread), diag_inverse, lower_blocks, sep_blocks],
    )
    high = within(spread, groups)
    far = [high, *gains_high, *gains_low, *finish_low, low1, low2, low3, couple, start, chain]
    shapes = [array.shape[1:] if 7 <= i < 10 else array.shape for i, array in enumerate(far)]
    solution, own = placed(
        backward_kernel,
        [shaped(rhs.shape, BF16), shaped((sep_width, columns), BF16)],
        [local_cols, sep_cols, core, own_level],
        far,
        [pltpu.VMEM(shape, array.dtype) for shape, array in zip(shapes, far)]
        + [
            pltpu.VMEM(rhs.shape, F32),
            pltpu.VMEM((count, columns, sep_width), BF16),
            pltpu.SemaphoreType.DMA((len(far),)),
        ],
    )
    return solution, own[None]


def solution(mesh):
    return jax.shard_map(
        per_device,
        mesh=mesh,
        in_specs=(
            P("blk", None, "cols"),
            P("blk", None, None),
            P("blk", None, None, None),
            P("blk", None),
            P("blk", None, "cols"),
            P("blk", None, None, None, None),
            P("blk", None, None),
            P("blk", None, None),
            P("blk", None, None),
        ),
        out_specs=(P("blk", None, "cols"), P("blk", None, "cols")),
        check_vma=False,
    )
```

```python
import jax
import jax.numpy as jnp
from jax import lax
from jax.experimental import pallas as pl
from jax.experimental.pallas import tpu as pltpu
from jax.sharding import PartitionSpec as P

F32 = jnp.float32
BF16 = jnp.bfloat16
PLANE_BITS = 4
LOW = 3


def dot(left, right):
    return jnp.dot(left, right, preferred_element_type=F32)


def dot_t(left, right):
    return lax.dot_general(left, right, (((0,), (0,)), ((), ())), preferred_element_type=F32)


def dot_nt(left, right):
    return lax.dot_general(left, right, (((1,), (1,)), ((), ())), preferred_element_type=F32)


def start_all(far, near, sems):
    copies = [pltpu.make_async_copy(far[i], near[i], sems.at[i]) for i in range(len(far))]
    for copy in copies:
        copy.start()
    return copies


def in_vmem(kernel, outs, scalars, arrays, scratch=()):
    counts = len(scalars), len(arrays), len(outs), len(arrays)

    def loaded(*refs):
        parts, first = [], 0
        for amount in counts:
            parts.append(refs[first : first + amount])
            first += amount
        small, far, results, near = parts
        for copy in start_all(far, near, refs[-1]):
            copy.wait()
        kernel(*small, *near, *results, *refs[first:-1])

    return placed(
        loaded,
        outs,
        scalars,
        arrays,
        [pltpu.VMEM(array.shape, array.dtype) for array in arrays]
        + list(scratch)
        + [pltpu.SemaphoreType.DMA((len(arrays),))],
    )


def placed(kernel, outs, scalars, arrays, scratch):
    vmem, smem = pl.BlockSpec(memory_space=pltpu.VMEM), pl.BlockSpec(memory_space=pltpu.SMEM)
    moved = sum(a.size * a.dtype.itemsize for a in arrays)
    moved += sum(o.size * o.dtype.itemsize for o in outs)
    return pl.pallas_call(
        kernel,
        out_shape=tuple(outs),
        in_specs=[smem] * len(scalars) + [pl.BlockSpec(memory_space=pl.ANY)] * len(arrays),
        out_specs=tuple(vmem for _ in outs),
        scratch_shapes=scratch,
        compiler_params=pltpu.CompilerParams(vmem_limit_bytes=56 * 2**20),
        cost_estimate=pl.CostEstimate(flops=10**9, bytes_accessed=moved, transcendentals=0),
    )(*scalars, *arrays)


def shaped(shape, dtype):
    return jax.ShapeDtypeStruct(shape, dtype)


def whole(core, mine, other, index):
    if mine.shape[1] == mine.shape[2]:
        return mine[index]
    first = core[0] == 0
    upper = jnp.where(first, mine[index], other[index])
    lower = jnp.where(first, other[index], mine[index])
    return jnp.concatenate([upper, lower], axis=0)


def gain_kernel(core, inverse, link, gain, finish, full):
    own = inverse[...]
    full[0] = dot(link[...], own).astype(BF16)
    full[1] = dot_t(own, own).astype(BF16)
    rows = gain.shape[0]
    first = pl.multiple_of(core[0] * rows, rows)
    gain[...] = full[0, pl.ds(first, rows)]
    finish[...] = full[1, pl.ds(first, rows)]


def spread_out(pieces, index, value):
    turned = value.T
    rows = pieces.shape[2]
    for piece in range(pieces.shape[0]):
        pieces[piece, index] = turned[piece * rows : (piece + 1) * rows]


def solve_rows(cols, first, inverse, lower, rhs, solved, folded, arrive):
    rows, width, _ = rhs.shape
    arrive(0)
    for row in range(rows):
        if first + row:
            pair = jnp.concatenate([lower[row, 0], lower[row, 1]], axis=1)
            folded[row] = dot(inverse[row], pair).astype(BF16)
    arrive(1)
    for row in range(rows):
        base = dot(inverse[row], rhs[row])
        if first + row:
            if row == 0:
                value = solved[first - 1]
                earlier = solved[cols[first, 1]]
            elif first + row == 1:
                earlier = value
            base = base - dot(folded[row, :, width:], earlier)
            base = base - dot(folded[row, :, :width], value)
        if row + 1 < rows and first + row:
            earlier = solved[cols[first + row + 1, 1]]
        value = base.astype(BF16)
        solved[first + row] = value


def first_kernel(cols, *refs):
    far, (solved,), near, (folded, sems) = refs[:3], refs[3:4], refs[4:7], refs[7:]
    rows = solved.shape[0]
    inverse, lower, rhs = near
    copies = start_all([ref.at[pl.ds(0, rows)] for ref in far], near, sems)

    def arrive(stage):
        for copy in copies[2:] if stage else copies[:2]:
            copy.wait()

    solve_rows(cols, 0, inverse, lower, rhs, solved, folded, arrive)


def second_kernel(cols, sep_cols, own_level, *refs):
    far, (solved, partial), near, (folded, sems) = refs[:6], refs[6:8], refs[8:13], refs[13:]
    inverse, lower, rhs, sep_blocks, sep_rhs = near
    rows = rhs.shape[0]
    views = [ref.at[pl.ds(rows, rows)] for ref in far[:3]] + list(far[3:5])
    copies = start_all(views + [far[5]], [*near, solved.at[pl.ds(0, rows)]], sems)

    def arrive(stage):
        for copy in (copies[2], copies[5]) if stage else copies[:2]:
            copy.wait()

    solve_rows(cols, rows, inverse, lower, rhs, solved, folded, arrive)
    copies[3].wait()
    copies[4].wait()
    for level in range(sep_blocks.shape[0]):
        pair = jnp.concatenate([sep_blocks[level, 0], sep_blocks[level, 1]], axis=1)
        sources = jnp.concatenate(
            [solved[sep_cols[level, 0]], solved[sep_cols[level, 1]]], axis=0
        )
        total = dot(pair, sources)
        partial[level] = total - jnp.where(own_level[0] == level, sep_rhs[...].astype(F32), 0.0)


def path_kernel(core, partial, mine, other, low, high):
    for level in range(partial.shape[0]):
        total = partial[level]
        if 1 <= level <= LOW:
            total = total - dot(whole(core, mine, other, level - 1), value)
        value = total.astype(BF16)
        if level < LOW:
            low[level] = value.T
        else:
            spread_out(high, level - LOW, value)


def plane_kernel(core, arrived, mine, other, fourth, above):
    sources = arrived.shape[0]
    value = sum(arrived[source, 0].astype(F32) for source in range(sources)).astype(BF16)
    fourth[...] = value
    for index in range(above.shape[1]):
        total = sum(arrived[source, index + 1].astype(F32) for source in range(sources))
        value = (total - dot_nt(value, whole(core, mine, other, index))).astype(BF16)
        for piece in range(above.shape[0]):
            above[piece, index] = value


def top_kernel(core, place, arrived, fourth, mine, other, spread):
    planes = arrived.shape[0]
    for level in range(spread.shape[1]):
        if level == 0:
            total = fourth[...]
        else:
            index = level - 1
            total = jnp.zeros(fourth.shape, F32)
            for source in range(planes):
                share = arrived[source, index].astype(F32)
                if 2 << index < planes:
                    near = (place[0] >> (index + 1)) == (source >> (index + 1))
                    share = jnp.where(near, share, 0.0)
                total = total + share
            total = total.astype(BF16)
        value = -dot(total, whole(core, mine, other, level))
        value = value.astype(BF16)
        for piece in range(spread.shape[0]):
            spread[piece, level] = value


def prepare_kernel(cols, sep_cols, solved, inverse, lower, sep_blocks, start, chain, couple):
    rows = solved.shape[0]
    for row in range(rows):
        start[row] = dot_t(inverse[row], solved[row])
    for row in range(1, rows):
        for slot in range(2):
            column = cols[row, slot] if slot else row - 1
            chain[row, slot] = dot(lower[row, slot], inverse[column]).astype(BF16).T
    for level in range(sep_blocks.shape[0]):
        for slot in range(2):
            product = dot(sep_blocks[level, slot], inverse[sep_cols[level, slot]])
            couple[level, slot] = product.astype(BF16).T


def backward_kernel(cols, sep_cols, core, own_level, *refs):
    far, (solution, own), near, (pending, nodes, sems) = (
        refs[:13],
        refs[13:15],
        refs[15:-3],
        refs[-3:],
    )
    far = far[:7] + tuple(stack.at[0] for stack in far[7:10]) + far[10:]
    copies = start_all(far, near, sems)
    high, gains_high, gains_high_other, gains_low, gains_low_other = near[:5]
    finish, finish_other = near[5:7]
    low = near[7:10]
    couple, start, chain = near[10:]
    rows = start.shape[0]
    count = nodes.shape[0]
    split = gains_low.shape[0]
    for copy in copies[:10]:
        copy.wait()
    for level in range(count - 1, -1, -1):
        if level < LOW:
            node = -dot(low[level][...], whole(core, finish, finish_other, level))
        else:
            pieces = [high[piece, level - LOW] for piece in range(high.shape[0])]
            node = jnp.concatenate(pieces, axis=0).astype(F32)
        if level + 1 < count:
            if level < split:
                gain = whole(core, gains_low, gains_low_other, level)
            else:
                gain = whole(core, gains_high, gains_high_other, level - split)
            node = node - dot(vector, gain)
        vector = node.astype(BF16)
        nodes[level] = vector
    own[...] = nodes[own_level[0]].T
    for copy in copies[10:]:
        copy.wait()
    pending[...] = start[...]
    for level in range(count - 1, -1, -1):
        for slot in range(2):
            column = sep_cols[level, slot]
            pending[column] = pending[column] - dot_nt(couple[level, slot], nodes[level])
    following = pending[rows - 1]
    for row in range(rows - 1, -1, -1):
        value = following.astype(BF16)
        solution[row] = value
        if row:
            following = pending[row - 1] - dot(chain[row, 0], value)
            if row > 1:
                column = cols[row, 1]
                pending[column] = pending[column] - dot(chain[row, 1], value)
            else:
                following = following - dot(chain[row, 1], value)


def other_core(mine):
    cores = lax.axis_size("cols")
    return lax.ppermute(mine, "cols", [(i, cores - 1 - i) for i in range(cores)])


def with_other_core(flags, pairs):
    mine = jnp.stack([jnp.where(flags[i] == 1, *pair[::-1]) for i, pair in enumerate(pairs)])
    return mine, other_core(mine)


def after(value, earlier):
    return lax.optimization_barrier((value, earlier))[0]


def per_device(
    rhs,
    diag_inverse,
    lower_blocks,
    local_cols,
    sep_rhs,
    sep_blocks,
    sep_cols,
    sep_inverse,
    sep_link,
):
    size = lax.axis_size("blk")
    device = lax.axis_index("blk")
    cores = lax.axis_size("cols")
    bits = size.bit_length() - 1
    count = bits + 1
    rows, width, columns = rhs.shape
    sep_width = sep_rhs.shape[1]
    plane = 1 << PLANE_BITS
    slice_rows = columns // plane
    sep_cols = sep_cols[0]
    sep_blocks = sep_blocks[0]
    own_level = sum(
        (((device + 1) & (2**k - 1)) == 0).astype(jnp.int32) for k in range(1, count)
    )[None]

    def step_mask(bit):
        base = 0 if bit < 2 else 2 if bit < 4 else 4
        return (2 << bit) - (1 << base)

    core = lax.axis_index("cols")[None]
    half = shaped((sep_width // cores, sep_width), BF16)
    gain, finish = in_vmem(
        gain_kernel,
        [half, half],
        [core],
        [sep_inverse[0], sep_link[0]],
        [pltpu.VMEM((2, sep_width, sep_width), BF16)],
    )

    flags = (device >> jnp.arange(count, dtype=jnp.int32)) & 1

    def climb(top, bit):
        mask = step_mask(bit)
        arrived = lax.ppermute(top, "blk", [(i, i ^ mask) for i in range(size)])
        return (top, arrived), jnp.where(flags[bit] == 1, top, arrived)

    piece = (slice_rows, sep_width)
    groups = [[g * plane + i for i in range(plane)] for g in range(size // plane)]
    towers = [[g + i * plane for i in range(size // plane)] for g in range(plane)]

    def within(value, members):
        return lax.all_to_all(value, "blk", 0, 0, axis_index_groups=members, tiled=True)

    half_rows = rows // 2
    halves = [
        pltpu.VMEM((half_rows, *array.shape[1:]), BF16)
        for array in (diag_inverse, lower_blocks, rhs)
    ]
    folded = pltpu.VMEM((half_rows, width, 2 * width), BF16)
    (solved_first,) = placed(
        first_kernel,
        [shaped((half_rows, width, columns), BF16)],
        [local_cols],
        [diag_inverse, lower_blocks, after(rhs, gain)],
        [*halves, folded, pltpu.SemaphoreType.DMA((3,))],
    )
    solved, partial = placed(
        second_kernel,
        [shaped(rhs.shape, BF16), shaped((count, sep_width, columns), F32)],
        [local_cols, sep_cols, own_level],
        [diag_inverse, lower_blocks, rhs, sep_blocks, sep_rhs[0], solved_first],
        [
            *halves,
            pltpu.VMEM(sep_blocks.shape, BF16),
            pltpu.VMEM(sep_rhs.shape[1:], BF16),
            folded,
            pltpu.SemaphoreType.DMA((6,)),
        ],
    )
    gain_list, finish_list = [], []

    def climb_gain(bit):
        nonlocal gain
        pair, gain = climb(gain, bit)
        gain_list.append(pair)

    def climb_finish(bit):
        nonlocal finish
        pair, finish = climb(finish, bit)
        finish_list.append(pair)

    def both(bit, event=None):
        nonlocal gain, finish
        finish = after(finish, gain)
        if event is not None:
            gain, finish = after(gain, event), after(finish, event)
        climb_gain(bit)
        climb_finish(bit - 1)

    climb_gain(0)
    both(1, solved_first)
    for bit in range(2, LOW):
        both(bit)
    gains_low = with_other_core(flags[:LOW], gain_list)
    both(LOW, solved)
    both(LOW + 1)
    low, shares = in_vmem(
        path_kernel,
        [shaped((LOW, columns, sep_width), BF16), shaped((plane, count - LOW, *piece), BF16)],
        [core],
        [partial, *gains_low],
    )
    both(LOW + 2, shares)
    arrived = within(shares, groups)

    def added(mine, other):
        return (mine.astype(F32) + other.astype(F32)).astype(BF16)

    def swapped(value, bit):
        mask = step_mask(bit)
        return added(value, lax.ppermute(value, "blk", [(i, i ^ mask) for i in range(size)]))

    low1 = swapped(after(low, arrived), 0)
    finish_low = with_other_core(flags[:LOW], finish_list[:LOW])
    both(LOW + 3, (arrived, finish_low))
    gains_high = with_other_core(flags[LOW:bits], gain_list[LOW:])
    climb_finish(bits - 1)
    finish_list.append((finish, finish))
    fourth, above = in_vmem(
        plane_kernel,
        [shaped(piece, BF16), shaped((size // plane, bits - LOW, *piece), BF16)],
        [core],
        [after(arrived, low1), *gains_high],
    )
    finish_high = with_other_core(flags[LOW:], finish_list[LOW:])
    low2 = swapped(low1[1:], 1)
    low3 = swapped(low2[1:], 2)
    arrived = after(within(above, towers), low3)
    (spread,) = in_vmem(
        top_kernel,
        [shaped((plane, count - LOW, *piece), BF16)],
        [core, (device >> PLANE_BITS)[None]],
        [arrived, fourth, *finish_high],
    )
    start, chain, couple = in_vmem(
        prepare_kernel,
        [
            shaped(rhs.shape, F32),
            shaped((rows, 2, width, width), BF16),
            shaped((count, 2, width, sep_width), BF16),
        ],
        [local_cols, sep_cols],
        [after(solved, spread), diag_inverse, lower_blocks, sep_blocks],
    )
    high = within(spread, groups)
    far = [high, *gains_high, *gains_low, *finish_low, low1, low2, low3, couple, start, chain]
    shapes = [array.shape[1:] if 7 <= i < 10 else array.shape for i, array in enumerate(far)]
    solution, own = placed(
        backward_kernel,
        [shaped(rhs.shape, BF16), shaped((sep_width, columns), BF16)],
        [local_cols, sep_cols, core, own_level],
        far,
        [pltpu.VMEM(shape, array.dtype) for shape, array in zip(shapes, far)]
        + [
            pltpu.VMEM(rhs.shape, F32),
            pltpu.VMEM((count, columns, sep_width), BF16),
            pltpu.SemaphoreType.DMA((len(far),)),
        ],
    )
    return solution, own[None]


def solution(mesh):
    return jax.shard_map(
        per_device,
        mesh=mesh,
        in_specs=(
            P("blk", None, "cols"),
            P("blk", None, None),
            P("blk", None, None, None),
            P("blk", None),
            P("blk", None, "cols"),
            P("blk", None, None, None, None),
            P("blk", None, None),
            P("blk", None, None),
            P("blk", None, None),
        ),
        out_specs=(P("blk", None, "cols"), P("blk", None, "cols")),
        check_vma=False,
    )
```

```python
import jax
import jax.numpy as jnp
from jax import lax
from jax.experimental import pallas as pl
from jax.experimental.pallas import tpu as pltpu
from jax.sharding import PartitionSpec as P

F32 = jnp.float32
BF16 = jnp.bfloat16
PLANE_BITS = 4
LOW = 3


def dot(left, right):
    return jnp.dot(left, right, preferred_element_type=F32)


def dot_t(left, right):
    return lax.dot_general(left, right, (((0,), (0,)), ((), ())), preferred_element_type=F32)


def dot_nt(left, right):
    return lax.dot_general(left, right, (((1,), (1,)), ((), ())), preferred_element_type=F32)


def start_all(far, near, sems):
    copies = [pltpu.make_async_copy(far[i], near[i], sems.at[i]) for i in range(len(far))]
    for copy in copies:
        copy.start()
    return copies


def start_picked(flags, pairs, near, sems):
    for index, (first, second) in enumerate(pairs):

        @pl.when(flags[index] == 0)
        def _():
            pltpu.make_async_copy(first, near.at[index], sems.at[index]).start()

        @pl.when(flags[index] != 0)
        def _():
            pltpu.make_async_copy(second, near.at[index], sems.at[index]).start()

    return [
        pltpu.make_async_copy(pair[0], near.at[index], sems.at[index])
        for index, pair in enumerate(pairs)
    ]


def in_vmem(kernel, outs, scalars, arrays, scratch=()):
    counts = len(scalars), len(arrays), len(outs), len(arrays)

    def loaded(*refs):
        parts, first = [], 0
        for amount in counts:
            parts.append(refs[first : first + amount])
            first += amount
        small, far, results, near = parts
        for copy in start_all(far, near, refs[-1]):
            copy.wait()
        kernel(*small, *near, *results, *refs[first:-1])

    return placed(
        loaded,
        outs,
        scalars,
        arrays,
        [pltpu.VMEM(array.shape, array.dtype) for array in arrays]
        + list(scratch)
        + [pltpu.SemaphoreType.DMA((len(arrays),))],
    )


def placed(kernel, outs, scalars, arrays, scratch):
    vmem, smem = pl.BlockSpec(memory_space=pltpu.VMEM), pl.BlockSpec(memory_space=pltpu.SMEM)
    moved = sum(a.size * a.dtype.itemsize for a in arrays)
    moved += sum(o.size * o.dtype.itemsize for o in outs)
    return pl.pallas_call(
        kernel,
        out_shape=tuple(outs),
        in_specs=[smem] * len(scalars) + [pl.BlockSpec(memory_space=pl.ANY)] * len(arrays),
        out_specs=tuple(vmem for _ in outs),
        scratch_shapes=scratch,
        compiler_params=pltpu.CompilerParams(vmem_limit_bytes=56 * 2**20),
        cost_estimate=pl.CostEstimate(flops=10**9, bytes_accessed=moved, transcendentals=0),
    )(*scalars, *arrays)


def shaped(shape, dtype):
    return jax.ShapeDtypeStruct(shape, dtype)


def whole(core, mine, other, index):
    if mine.shape[1] == mine.shape[2]:
        return mine[index]
    first = core[0] == 0
    upper = jnp.where(first, mine[index], other[index])
    lower = jnp.where(first, other[index], mine[index])
    return jnp.concatenate([upper, lower], axis=0)


def gain_kernel(core, inverse, link, gain, finish, full):
    own = inverse[...]
    full[...] = dot(link[...], own).astype(BF16)
    rows = gain.shape[0]
    gain[...] = full[pl.ds(pl.multiple_of(core[0] * rows, rows), rows)]
    finish[...] = dot_t(own, own).astype(BF16)


def spread_out(pieces, index, value):
    turned = value.T
    rows = pieces.shape[2]
    for piece in range(pieces.shape[0]):
        pieces[piece, index] = turned[piece * rows : (piece + 1) * rows]


def solve_rows(cols, first, inverse, lower, rhs, solved, folded, arrive):
    rows, width, _ = rhs.shape
    arrive(0)
    for row in range(rows):
        if first + row:
            pair = jnp.concatenate([lower[row, 0], lower[row, 1]], axis=1)
            folded[row] = dot(inverse[row], pair).astype(BF16)
    arrive(1)
    for row in range(rows):
        base = dot(inverse[row], rhs[row])
        if first + row:
            if row == 0:
                value = solved[first - 1]
                earlier = solved[cols[first, 1]]
            elif first + row == 1:
                earlier = value
            base = base - dot(folded[row, :, width:], earlier)
            base = base - dot(folded[row, :, :width], value)
        if row + 1 < rows and first + row:
            earlier = solved[cols[first + row + 1, 1]]
        value = base.astype(BF16)
        solved[first + row] = value


def first_kernel(cols, *refs):
    far, (solved,), near, (folded, sems) = refs[:3], refs[3:4], refs[4:7], refs[7:]
    rows = solved.shape[0]
    inverse, lower, rhs = near
    copies = start_all([ref.at[pl.ds(0, rows)] for ref in far], near, sems)

    def arrive(stage):
        for copy in copies[2:] if stage else copies[:2]:
            copy.wait()

    solve_rows(cols, 0, inverse, lower, rhs, solved, folded, arrive)


def second_kernel(cols, sep_cols, own_level, *refs):
    far, (solved, partial), near, (folded, sems) = refs[:6], refs[6:8], refs[8:13], refs[13:]
    inverse, lower, rhs, sep_blocks, sep_rhs = near
    rows = rhs.shape[0]
    views = [ref.at[pl.ds(rows, rows)] for ref in far[:3]] + list(far[3:5])
    copies = start_all(views + [far[5]], [*near, solved.at[pl.ds(0, rows)]], sems)

    def arrive(stage):
        for copy in (copies[2], copies[5]) if stage else copies[:2]:
            copy.wait()

    solve_rows(cols, rows, inverse, lower, rhs, solved, folded, arrive)
    copies[3].wait()
    copies[4].wait()
    for level in range(sep_blocks.shape[0]):
        pair = jnp.concatenate([sep_blocks[level, 0], sep_blocks[level, 1]], axis=1)
        sources = jnp.concatenate(
            [solved[sep_cols[level, 0]], solved[sep_cols[level, 1]]], axis=0
        )
        total = dot(pair, sources)
        partial[level] = total - jnp.where(own_level[0] == level, sep_rhs[...].astype(F32), 0.0)


def path_kernel(core, partial, mine, other, low, high):
    for level in range(partial.shape[0]):
        total = partial[level]
        if 1 <= level <= LOW:
            total = total - dot(whole(core, mine, other, level - 1), value)
        value = total.astype(BF16)
        if level < LOW:
            low[level] = value.T
        else:
            spread_out(high, level - LOW, value)


def plane_kernel(core, arrived, mine, other, fourth, above):
    sources = arrived.shape[0]
    value = sum(arrived[source, 0].astype(F32) for source in range(sources)).astype(BF16)
    fourth[...] = value
    for index in range(above.shape[1]):
        total = sum(arrived[source, index + 1].astype(F32) for source in range(sources))
        value = (total - dot_nt(value, whole(core, mine, other, index))).astype(BF16)
        for piece in range(above.shape[0]):
            above[piece, index] = value


def top_kernel(place, flags, *refs):
    far, spread, (arrived, fourth, finish, sems) = refs[:-5], refs[-5], refs[-4:]
    copies = start_all(far[:2], (arrived, fourth), sems)
    pairs = list(zip(far[2::2], far[3::2]))
    copies += start_picked(flags, pairs, finish, sems.at[pl.ds(2, len(pairs))])
    for copy in copies:
        copy.wait()
    planes = arrived.shape[0]
    for level in range(spread.shape[1]):
        if level == 0:
            total = fourth[...]
        else:
            index = level - 1
            total = jnp.zeros(fourth.shape, F32)
            for source in range(planes):
                share = arrived[source, index].astype(F32)
                if 2 << index < planes:
                    near = (place[0] >> (index + 1)) == (source >> (index + 1))
                    share = jnp.where(near, share, 0.0)
                total = total + share
            total = total.astype(BF16)
        value = -dot(total, finish[level])
        value = value.astype(BF16)
        for piece in range(spread.shape[0]):
            spread[piece, level] = value


def prepare_kernel(cols, sep_cols, solved, inverse, lower, sep_blocks, start, chain, couple):
    rows = solved.shape[0]
    for row in range(rows):
        start[row] = dot_t(inverse[row], solved[row])
    for row in range(1, rows):
        for slot in range(2):
            column = cols[row, slot] if slot else row - 1
            chain[row, slot] = dot(lower[row, slot], inverse[column]).astype(BF16).T
    for level in range(sep_blocks.shape[0]):
        for slot in range(2):
            product = dot(sep_blocks[level, slot], inverse[sep_cols[level, slot]])
            couple[level, slot] = product.astype(BF16).T


def backward_kernel(cols, sep_cols, core, own_level, flags, *refs):
    far, (solution, own), near, (finish, pending, nodes, sems) = (
        refs[:17],
        refs[17:19],
        refs[19:-4],
        refs[-4:],
    )
    direct = far[:5] + tuple(stack.at[0] for stack in far[5:8]) + far[8:11]
    copies = start_all(direct[:8], near[:8], sems)
    pairs = list(zip(far[11::2], far[12::2]))
    copies += start_picked(flags, pairs, finish, sems.at[pl.ds(11, LOW)])
    later = start_all(direct[8:], near[8:], sems.at[pl.ds(8, 3)])
    high, gains_high, gains_high_other, gains_low, gains_low_other = near[:5]
    low = near[5:8]
    couple, start, chain = near[8:]
    rows = start.shape[0]
    count = nodes.shape[0]
    split = gains_low.shape[0]
    for copy in copies:
        copy.wait()
    for level in range(count - 1, -1, -1):
        if level < LOW:
            node = -dot(low[level][...], finish[level])
        else:
            pieces = [high[piece, level - LOW] for piece in range(high.shape[0])]
            node = jnp.concatenate(pieces, axis=0).astype(F32)
        if level + 1 < count:
            if level < split:
                gain = whole(core, gains_low, gains_low_other, level)
            else:
                gain = whole(core, gains_high, gains_high_other, level - split)
            node = node - dot(vector, gain)
        vector = node.astype(BF16)
        nodes[level] = vector
    own[...] = nodes[own_level[0]].T
    for copy in later:
        copy.wait()
    pending[...] = start[...]
    for level in range(count - 1, -1, -1):
        for slot in range(2):
            column = sep_cols[level, slot]
            pending[column] = pending[column] - dot_nt(couple[level, slot], nodes[level])
    following = pending[rows - 1]
    for row in range(rows - 1, -1, -1):
        value = following.astype(BF16)
        solution[row] = value
        if row:
            following = pending[row - 1] - dot(chain[row, 0], value)
            if row > 1:
                column = cols[row, 1]
                pending[column] = pending[column] - dot(chain[row, 1], value)
            else:
                following = following - dot(chain[row, 1], value)


def other_core(mine):
    cores = lax.axis_size("cols")
    return lax.ppermute(mine, "cols", [(i, cores - 1 - i) for i in range(cores)])


def with_other_core(flags, pairs):
    mine = jnp.stack([jnp.where(flags[i] == 1, *pair[::-1]) for i, pair in enumerate(pairs)])
    return mine, other_core(mine)


def after(value, earlier):
    return lax.optimization_barrier((value, earlier))[0]


def per_device(
    rhs,
    diag_inverse,
    lower_blocks,
    local_cols,
    sep_rhs,
    sep_blocks,
    sep_cols,
    sep_inverse,
    sep_link,
):
    size = lax.axis_size("blk")
    device = lax.axis_index("blk")
    cores = lax.axis_size("cols")
    bits = size.bit_length() - 1
    count = bits + 1
    rows, width, columns = rhs.shape
    sep_width = sep_rhs.shape[1]
    plane = 1 << PLANE_BITS
    slice_rows = columns // plane
    sep_cols = sep_cols[0]
    sep_blocks = sep_blocks[0]
    own_level = sum(
        (((device + 1) & (2**k - 1)) == 0).astype(jnp.int32) for k in range(1, count)
    )[None]

    def step_mask(bit):
        base = 0 if bit < 2 else 2 if bit < 4 else 4
        return (2 << bit) - (1 << base)

    core = lax.axis_index("cols")[None]
    gain, finish = in_vmem(
        gain_kernel,
        [shaped((sep_width // cores, sep_width), BF16), shaped((sep_width, sep_width), BF16)],
        [core],
        [sep_inverse[0], sep_link[0]],
        [pltpu.VMEM((sep_width, sep_width), BF16)],
    )

    flags = (device >> jnp.arange(count, dtype=jnp.int32)) & 1

    def climb(top, bit):
        mask = step_mask(bit)
        arrived = lax.ppermute(top, "blk", [(i, i ^ mask) for i in range(size)])
        return (top, arrived), jnp.where(flags[bit] == 1, top, arrived)

    piece = (slice_rows, sep_width)
    groups = [[g * plane + i for i in range(plane)] for g in range(size // plane)]
    towers = [[g + i * plane for i in range(size // plane)] for g in range(plane)]

    def within(value, members):
        return lax.all_to_all(value, "blk", 0, 0, axis_index_groups=members, tiled=True)

    half_rows = rows // 2
    halves = [
        pltpu.VMEM((half_rows, *array.shape[1:]), BF16)
        for array in (diag_inverse, lower_blocks, rhs)
    ]
    folded = pltpu.VMEM((half_rows, width, 2 * width), BF16)
    (solved_first,) = placed(
        first_kernel,
        [shaped((half_rows, width, columns), BF16)],
        [local_cols],
        [diag_inverse, lower_blocks, after(rhs, gain)],
        [*halves, folded, pltpu.SemaphoreType.DMA((3,))],
    )
    solved, partial = placed(
        second_kernel,
        [shaped(rhs.shape, BF16), shaped((count, sep_width, columns), F32)],
        [local_cols, sep_cols, own_level],
        [diag_inverse, lower_blocks, rhs, sep_blocks, sep_rhs[0], solved_first],
        [
            *halves,
            pltpu.VMEM(sep_blocks.shape, BF16),
            pltpu.VMEM(sep_rhs.shape[1:], BF16),
            folded,
            pltpu.SemaphoreType.DMA((6,)),
        ],
    )
    gain_list, finish_list = [], []

    def climb_gain(bit):
        nonlocal gain
        pair, gain = climb(gain, bit)
        gain_list.append(pair)

    def climb_finish(bit):
        nonlocal finish
        pair, finish = climb(finish, bit)
        finish_list.append(pair)

    def both(bit):
        nonlocal finish
        finish = after(finish, gain)
        climb_gain(bit)
        climb_finish(bit - 1)

    climb_gain(0)
    gain = after(gain, solved_first)
    both(1)
    both(2)
    gains_low = with_other_core(flags[:LOW], gain_list)
    both(LOW)
    low, shares = in_vmem(
        path_kernel,
        [shaped((LOW, columns, sep_width), BF16), shaped((plane, count - LOW, *piece), BF16)],
        [core],
        [partial, *gains_low],
    )
    arrived = within(shares, groups)
    gain = after(gain, shares)
    both(LOW + 1)
    both(LOW + 2)
    both(LOW + 3)

    def added(mine, other):
        return (mine.astype(F32) + other.astype(F32)).astype(BF16)

    def swapped(value, bit):
        mask = step_mask(bit)
        return added(value, lax.ppermute(value, "blk", [(i, i ^ mask) for i in range(size)]))

    low1 = swapped(after(low, arrived), 0)
    low2 = swapped(low1[1:], 1)
    low3 = swapped(low2[1:], 2)
    gain_list[-1] = after(gain_list[-1], arrived)
    gains_high = with_other_core(flags[LOW:bits], gain_list[LOW:])
    finish = after(finish, gain)
    climb_finish(bits - 1)
    finish_list.append((finish, finish))
    fourth, above = in_vmem(
        plane_kernel,
        [shaped(piece, BF16), shaped((size // plane, bits - LOW, *piece), BF16)],
        [core],
        [arrived, *gains_high],
    )
    arrived = after(within(above, towers), low3)
    matrix = (sep_width, sep_width)
    (spread,) = placed(
        top_kernel,
        [shaped((plane, count - LOW, *piece), BF16)],
        [(device >> PLANE_BITS)[None], flags[LOW:]],
        [arrived, fourth, *[array for pair in finish_list[LOW:] for array in pair]],
        [
            pltpu.VMEM(arrived.shape, BF16),
            pltpu.VMEM(piece, BF16),
            pltpu.VMEM((count - LOW, *matrix), BF16),
            pltpu.SemaphoreType.DMA((2 + count - LOW,)),
        ],
    )
    start, chain, couple = in_vmem(
        prepare_kernel,
        [
            shaped(rhs.shape, F32),
            shaped((rows, 2, width, width), BF16),
            shaped((count, 2, width, sep_width), BF16),
        ],
        [local_cols, sep_cols],
        [after(solved, spread), diag_inverse, lower_blocks, sep_blocks],
    )
    high = within(spread, groups)
    far = [high, *gains_high, *gains_low, low1, low2, low3, couple, start, chain]
    shapes = [array.shape[1:] if 5 <= i < 8 else array.shape for i, array in enumerate(far)]
    solution, own = placed(
        backward_kernel,
        [shaped(rhs.shape, BF16), shaped((sep_width, columns), BF16)],
        [local_cols, sep_cols, core, own_level, flags],
        far + [array for pair in finish_list[:LOW] for array in pair],
        [pltpu.VMEM(shape, array.dtype) for shape, array in zip(shapes, far)]
        + [
            pltpu.VMEM((LOW, *matrix), BF16),
            pltpu.VMEM(rhs.shape, F32),
            pltpu.VMEM((count, columns, sep_width), BF16),
            pltpu.SemaphoreType.DMA((len(far) + LOW,)),
        ],
    )
    return solution, own[None]


def solution(mesh):
    return jax.shard_map(
        per_device,
        mesh=mesh,
        in_specs=(
            P("blk", None, "cols"),
            P("blk", None, None),
            P("blk", None, None, None),
            P("blk", None),
            P("blk", None, "cols"),
            P("blk", None, None, None, None),
            P("blk", None, None),
            P("blk", None, None),
            P("blk", None, None),
        ),
        out_specs=(P("blk", None, "cols"), P("blk", None, "cols")),
        check_vma=False,
    )
```

```python
import jax
import jax.numpy as jnp
from jax import lax
from jax.experimental import pallas as pl
from jax.experimental.pallas import tpu as pltpu
from jax.sharding import PartitionSpec as P

F32 = jnp.float32
BF16 = jnp.bfloat16
PLANE_BITS = 4
LOW = 3


def dot(left, right):
    return jnp.dot(left, right, preferred_element_type=F32)


def dot_t(left, right):
    return lax.dot_general(left, right, (((0,), (0,)), ((), ())), preferred_element_type=F32)


def dot_nt(left, right):
    return lax.dot_general(left, right, (((1,), (1,)), ((), ())), preferred_element_type=F32)


def start_all(far, near, sems):
    copies = [pltpu.make_async_copy(far[i], near[i], sems.at[i]) for i in range(len(far))]
    for copy in copies:
        copy.start()
    return copies


def start_picked(flags, pairs, near, sems):
    for index, (first, second) in enumerate(pairs):

        @pl.when(flags[index] == 0)
        def _():
            pltpu.make_async_copy(first, near.at[index], sems.at[index]).start()

        @pl.when(flags[index] != 0)
        def _():
            pltpu.make_async_copy(second, near.at[index], sems.at[index]).start()

    return [
        pltpu.make_async_copy(pair[0], near.at[index], sems.at[index])
        for index, pair in enumerate(pairs)
    ]


def in_vmem(kernel, outs, scalars, arrays, scratch=()):
    counts = len(scalars), len(arrays), len(outs), len(arrays)

    def loaded(*refs):
        parts, first = [], 0
        for amount in counts:
            parts.append(refs[first : first + amount])
            first += amount
        small, far, results, near = parts
        for copy in start_all(far, near, refs[-1]):
            copy.wait()
        kernel(*small, *near, *results, *refs[first:-1])

    return placed(
        loaded,
        outs,
        scalars,
        arrays,
        [pltpu.VMEM(array.shape, array.dtype) for array in arrays]
        + list(scratch)
        + [pltpu.SemaphoreType.DMA((len(arrays),))],
    )


def placed(kernel, outs, scalars, arrays, scratch):
    vmem, smem = pl.BlockSpec(memory_space=pltpu.VMEM), pl.BlockSpec(memory_space=pltpu.SMEM)
    moved = sum(a.size * a.dtype.itemsize for a in arrays)
    moved += sum(o.size * o.dtype.itemsize for o in outs)
    return pl.pallas_call(
        kernel,
        out_shape=tuple(outs),
        in_specs=[smem] * len(scalars) + [pl.BlockSpec(memory_space=pl.ANY)] * len(arrays),
        out_specs=tuple(vmem for _ in outs),
        scratch_shapes=scratch,
        compiler_params=pltpu.CompilerParams(vmem_limit_bytes=56 * 2**20),
        cost_estimate=pl.CostEstimate(flops=10**9, bytes_accessed=moved, transcendentals=0),
    )(*scalars, *arrays)


def shaped(shape, dtype):
    return jax.ShapeDtypeStruct(shape, dtype)


def whole(core, mine, other, index):
    if mine.shape[1] == mine.shape[2]:
        return mine[index]
    first = core[0] == 0
    upper = jnp.where(first, mine[index], other[index])
    lower = jnp.where(first, other[index], mine[index])
    return jnp.concatenate([upper, lower], axis=0)


def gain_kernel(core, inverse, link, gain, finish, full):
    own = inverse[...]
    full[...] = dot(link[...], own).astype(BF16)
    rows = gain.shape[0]
    gain[...] = full[pl.ds(pl.multiple_of(core[0] * rows, rows), rows)]
    finish[...] = dot_t(own, own).astype(BF16)


def spread_out(pieces, index, value):
    turned = value.T
    rows = pieces.shape[2]
    for piece in range(pieces.shape[0]):
        pieces[piece, index] = turned[piece * rows : (piece + 1) * rows]


def solve_rows(cols, first, inverse, lower, rhs, solved, folded, arrive):
    rows, width, _ = rhs.shape
    arrive(0)
    for row in range(rows):
        if first + row:
            pair = jnp.concatenate([lower[row, 0], lower[row, 1]], axis=1)
            folded[row] = dot(inverse[row], pair).astype(BF16)
    arrive(1)
    for row in range(rows):
        base = dot(inverse[row], rhs[row])
        if first + row:
            if row == 0:
                value = solved[first - 1]
                earlier = solved[cols[first, 1]]
            elif first + row == 1:
                earlier = value
            base = base - dot(folded[row, :, width:], earlier)
            base = base - dot(folded[row, :, :width], value)
        if row + 1 < rows and first + row:
            earlier = solved[cols[first + row + 1, 1]]
        value = base.astype(BF16)
        solved[first + row] = value


def first_kernel(cols, *refs):
    far, (solved,), near, (folded, sems) = refs[:3], refs[3:4], refs[4:7], refs[7:]
    rows = solved.shape[0]
    inverse, lower, rhs = near
    copies = start_all([ref.at[pl.ds(0, rows)] for ref in far], near, sems)

    def arrive(stage):
        for copy in copies[2:] if stage else copies[:2]:
            copy.wait()

    solve_rows(cols, 0, inverse, lower, rhs, solved, folded, arrive)


def second_kernel(cols, sep_cols, own_level, *refs):
    far, (solved, partial), near, (folded, sems) = refs[:6], refs[6:8], refs[8:13], refs[13:]
    inverse, lower, rhs, sep_blocks, sep_rhs = near
    rows = rhs.shape[0]
    views = [ref.at[pl.ds(rows, rows)] for ref in far[:3]] + list(far[3:5])
    copies = start_all(views + [far[5]], [*near, solved.at[pl.ds(0, rows)]], sems)

    def arrive(stage):
        for copy in (copies[2], copies[5]) if stage else copies[:2]:
            copy.wait()

    solve_rows(cols, rows, inverse, lower, rhs, solved, folded, arrive)
    copies[3].wait()
    copies[4].wait()
    for level in range(sep_blocks.shape[0]):
        pair = jnp.concatenate([sep_blocks[level, 0], sep_blocks[level, 1]], axis=1)
        sources = jnp.concatenate(
            [solved[sep_cols[level, 0]], solved[sep_cols[level, 1]]], axis=0
        )
        total = dot(pair, sources)
        partial[level] = total - jnp.where(own_level[0] == level, sep_rhs[...].astype(F32), 0.0)


def path_kernel(core, partial, mine, other, low, high):
    for level in range(partial.shape[0]):
        total = partial[level]
        if 1 <= level <= LOW:
            total = total - dot(whole(core, mine, other, level - 1), value)
        value = total.astype(BF16)
        if level < LOW:
            low[level] = value.T
        else:
            spread_out(high, level - LOW, value)


def plane_kernel(core, arrived, mine, other, fourth, above):
    sources = arrived.shape[0]
    value = sum(arrived[source, 0].astype(F32) for source in range(sources)).astype(BF16)
    fourth[...] = value
    for index in range(above.shape[1]):
        total = sum(arrived[source, index + 1].astype(F32) for source in range(sources))
        value = (total - dot_nt(value, whole(core, mine, other, index))).astype(BF16)
        for piece in range(above.shape[0]):
            above[piece, index] = value


def top_kernel(place, flags, *refs):
    far, spread, (arrived, fourth, finish, sems) = refs[:-5], refs[-5], refs[-4:]
    copies = start_all(far[:2], (arrived, fourth), sems)
    pairs = list(zip(far[2::2], far[3::2]))
    copies += start_picked(flags, pairs, finish, sems.at[pl.ds(2, len(pairs))])
    for copy in copies:
        copy.wait()
    planes = arrived.shape[0]
    for level in range(spread.shape[1]):
        if level == 0:
            total = fourth[...]
        else:
            index = level - 1
            total = jnp.zeros(fourth.shape, F32)
            for source in range(planes):
                share = arrived[source, index].astype(F32)
                if 2 << index < planes:
                    near = (place[0] >> (index + 1)) == (source >> (index + 1))
                    share = jnp.where(near, share, 0.0)
                total = total + share
            total = total.astype(BF16)
        value = -dot(total, finish[level])
        value = value.astype(BF16)
        for piece in range(spread.shape[0]):
            spread[piece, level] = value


def prepare_kernel(cols, sep_cols, solved, inverse, lower, sep_blocks, start, chain, couple):
    rows = solved.shape[0]
    for row in range(rows):
        start[row] = dot_t(inverse[row], solved[row])
    for row in range(1, rows):
        for slot in range(2):
            column = cols[row, slot] if slot else row - 1
            chain[row, slot] = dot(lower[row, slot], inverse[column]).astype(BF16).T
    for level in range(sep_blocks.shape[0]):
        for slot in range(2):
            product = dot(sep_blocks[level, slot], inverse[sep_cols[level, slot]])
            couple[level, slot] = product.astype(BF16).T


def backward_kernel(cols, sep_cols, core, own_level, flags, *refs):
    far, (solution, own), near, (finish, pending, nodes, sems) = (
        refs[:17],
        refs[17:19],
        refs[19:-4],
        refs[-4:],
    )
    direct = far[:5] + tuple(stack.at[0] for stack in far[5:8]) + far[8:11]
    copies = start_all(direct[:8], near[:8], sems)
    pairs = list(zip(far[11::2], far[12::2]))
    copies += start_picked(flags, pairs, finish, sems.at[pl.ds(11, LOW)])
    later = start_all(direct[8:], near[8:], sems.at[pl.ds(8, 3)])
    high, gains_high, gains_high_other, gains_low, gains_low_other = near[:5]
    low = near[5:8]
    couple, start, chain = near[8:]
    rows = start.shape[0]
    count = nodes.shape[0]
    split = gains_low.shape[0]
    for copy in copies:
        copy.wait()
    for level in range(count - 1, -1, -1):
        if level < LOW:
            node = -dot(low[level][...], finish[level])
        else:
            pieces = [high[piece, level - LOW] for piece in range(high.shape[0])]
            node = jnp.concatenate(pieces, axis=0).astype(F32)
        if level + 1 < count:
            if level < split:
                gain = whole(core, gains_low, gains_low_other, level)
            else:
                gain = whole(core, gains_high, gains_high_other, level - split)
            node = node - dot(vector, gain)
        vector = node.astype(BF16)
        nodes[level] = vector
    own[...] = nodes[own_level[0]].T
    for copy in later:
        copy.wait()
    pending[...] = start[...]
    for level in range(count - 1, -1, -1):
        for slot in range(2):
            column = sep_cols[level, slot]
            pending[column] = pending[column] - dot_nt(couple[level, slot], nodes[level])
    following = pending[rows - 1]
    for row in range(rows - 1, -1, -1):
        value = following.astype(BF16)
        solution[row] = value
        if row:
            following = pending[row - 1] - dot(chain[row, 0], value)
            if row > 1:
                column = cols[row, 1]
                pending[column] = pending[column] - dot(chain[row, 1], value)
            else:
                following = following - dot(chain[row, 1], value)


def other_core(mine):
    cores = lax.axis_size("cols")
    return lax.ppermute(mine, "cols", [(i, cores - 1 - i) for i in range(cores)])


def with_other_core(flags, pairs):
    mine = jnp.stack([jnp.where(flags[i] == 1, *pair[::-1]) for i, pair in enumerate(pairs)])
    return mine, other_core(mine)


def after(value, earlier):
    return lax.optimization_barrier((value, earlier))[0]


def per_device(
    rhs,
    diag_inverse,
    lower_blocks,
    local_cols,
    sep_rhs,
    sep_blocks,
    sep_cols,
    sep_inverse,
    sep_link,
):
    size = lax.axis_size("blk")
    device = lax.axis_index("blk")
    cores = lax.axis_size("cols")
    bits = size.bit_length() - 1
    count = bits + 1
    rows, width, columns = rhs.shape
    sep_width = sep_rhs.shape[1]
    plane = 1 << PLANE_BITS
    slice_rows = columns // plane
    sep_cols = sep_cols[0]
    sep_blocks = sep_blocks[0]
    own_level = sum(
        (((device + 1) & (2**k - 1)) == 0).astype(jnp.int32) for k in range(1, count)
    )[None]

    def step_mask(bit):
        base = 0 if bit < 2 else 2 if bit < 4 else 4
        return (2 << bit) - (1 << base)

    core = lax.axis_index("cols")[None]
    gain, finish = in_vmem(
        gain_kernel,
        [shaped((sep_width // cores, sep_width), BF16), shaped((sep_width, sep_width), BF16)],
        [core],
        [sep_inverse[0], sep_link[0]],
        [pltpu.VMEM((sep_width, sep_width), BF16)],
    )

    flags = (device >> jnp.arange(count, dtype=jnp.int32)) & 1

    def climb(top, bit):
        mask = step_mask(bit)
        arrived = lax.ppermute(top, "blk", [(i, i ^ mask) for i in range(size)])
        return (top, arrived), jnp.where(flags[bit] == 1, top, arrived)

    piece = (slice_rows, sep_width)
    groups = [[g * plane + i for i in range(plane)] for g in range(size // plane)]
    towers = [[g + i * plane for i in range(size // plane)] for g in range(plane)]

    def within(value, members):
        return lax.all_to_all(value, "blk", 0, 0, axis_index_groups=members, tiled=True)

    half_rows = rows // 2
    halves = [
        pltpu.VMEM((half_rows, *array.shape[1:]), BF16)
        for array in (diag_inverse, lower_blocks, rhs)
    ]
    folded = pltpu.VMEM((half_rows, width, 2 * width), BF16)
    (solved_first,) = placed(
        first_kernel,
        [shaped((half_rows, width, columns), BF16)],
        [local_cols],
        [diag_inverse, lower_blocks, after(rhs, gain)],
        [*halves, folded, pltpu.SemaphoreType.DMA((3,))],
    )
    solved, partial = placed(
        second_kernel,
        [shaped(rhs.shape, BF16), shaped((count, sep_width, columns), F32)],
        [local_cols, sep_cols, own_level],
        [diag_inverse, lower_blocks, rhs, sep_blocks, sep_rhs[0], solved_first],
        [
            *halves,
            pltpu.VMEM(sep_blocks.shape, BF16),
            pltpu.VMEM(sep_rhs.shape[1:], BF16),
            folded,
            pltpu.SemaphoreType.DMA((6,)),
        ],
    )
    gain_list, finish_list = [], []

    def climb_gain(bit):
        nonlocal gain
        pair, gain = climb(gain, bit)
        gain_list.append(pair)

    def climb_finish(bit):
        nonlocal finish
        pair, finish = climb(finish, bit)
        finish_list.append(pair)

    def both(bit):
        nonlocal finish
        finish = after(finish, gain)
        climb_gain(bit)
        climb_finish(bit - 1)

    climb_gain(0)
    gain = after(gain, solved_first)
    both(1)
    both(2)
    gains_low = with_other_core(flags[:LOW], gain_list)
    both(LOW)
    low, shares = in_vmem(
        path_kernel,
        [shaped((LOW, columns, sep_width), BF16), shaped((plane, count - LOW, *piece), BF16)],
        [core],
        [partial, *gains_low],
    )
    arrived = within(shares, groups)
    gain = after(gain, shares)
    both(LOW + 1)
    both(LOW + 2)
    both(LOW + 3)

    def added(mine, other):
        return (mine.astype(F32) + other.astype(F32)).astype(BF16)

    def swapped(value, bit):
        mask = step_mask(bit)
        return added(value, lax.ppermute(value, "blk", [(i, i ^ mask) for i in range(size)]))

    low1 = swapped(after(low, arrived), 0)
    gain_list[-1] = after(gain_list[-1], arrived)
    gains_high = with_other_core(flags[LOW:bits], gain_list[LOW:])
    finish = after(finish, gain)
    climb_finish(bits - 1)
    finish_list.append((finish, finish))
    fourth, above = in_vmem(
        plane_kernel,
        [shaped(piece, BF16), shaped((size // plane, bits - LOW, *piece), BF16)],
        [core],
        [arrived, *gains_high],
    )
    low2 = swapped(after(low1[1:], above), 1)
    arrived = after(within(above, towers), low2)
    matrix = (sep_width, sep_width)
    (spread,) = placed(
        top_kernel,
        [shaped((plane, count - LOW, *piece), BF16)],
        [(device >> PLANE_BITS)[None], flags[LOW:]],
        [arrived, fourth, *[array for pair in finish_list[LOW:] for array in pair]],
        [
            pltpu.VMEM(arrived.shape, BF16),
            pltpu.VMEM(piece, BF16),
            pltpu.VMEM((count - LOW, *matrix), BF16),
            pltpu.SemaphoreType.DMA((2 + count - LOW,)),
        ],
    )
    low3 = swapped(after(low2[1:], spread), 2)
    start, chain, couple = in_vmem(
        prepare_kernel,
        [
            shaped(rhs.shape, F32),
            shaped((rows, 2, width, width), BF16),
            shaped((count, 2, width, sep_width), BF16),
        ],
        [local_cols, sep_cols],
        [after(solved, spread), diag_inverse, lower_blocks, sep_blocks],
    )
    high = within(spread, groups)
    far = [high, *gains_high, *gains_low, low1, low2, low3, couple, start, chain]
    shapes = [array.shape[1:] if 5 <= i < 8 else array.shape for i, array in enumerate(far)]
    solution, own = placed(
        backward_kernel,
        [shaped(rhs.shape, BF16), shaped((sep_width, columns), BF16)],
        [local_cols, sep_cols, core, own_level, flags],
        far + [array for pair in finish_list[:LOW] for array in pair],
        [pltpu.VMEM(shape, array.dtype) for shape, array in zip(shapes, far)]
        + [
            pltpu.VMEM((LOW, *matrix), BF16),
            pltpu.VMEM(rhs.shape, F32),
            pltpu.VMEM((count, columns, sep_width), BF16),
            pltpu.SemaphoreType.DMA((len(far) + LOW,)),
        ],
    )
    return solution, own[None]


def solution(mesh):
    return jax.shard_map(
        per_device,
        mesh=mesh,
        in_specs=(
            P("blk", None, "cols"),
            P("blk", None, None),
            P("blk", None, None, None),
            P("blk", None),
            P("blk", None, "cols"),
            P("blk", None, None, None, None),
            P("blk", None, None),
            P("blk", None, None),
            P("blk", None, None),
        ),
        out_specs=(P("blk", None, "cols"), P("blk", None, "cols")),
        check_vma=False,
    )
```
